32 devices in a mesh: ctx: 8 (over z, y), head: 4 (over x, core).
Axes of the slice: x: 2, y: 2, z: 4, core: 2. Of those that a mesh axis runs over, the one named last changes fastest.
Arguments:
- tokens: bfloat16 [4096, 2560], P('ctx', 'head'), may hold values from -6 to 6
- tangent_tokens: bfloat16 [4096, 2560], P('ctx', 'head'), may hold values from -6 to 6
- log_decay: float32 [4096, 80], P('ctx', 'head'), may hold values from -1.5 to 0, as said below
- tangent_decay: float32 [4096, 80], P('ctx', 'head'), may hold values from -0.096 to 0.096
- w_inner: bfloat16 [2560, 5120], P(None, 'head'), may hold values from -0.125 to 0.125
- w_bmat: bfloat16 [2560, 128], replicated, may hold values from -0.00390625 to 0.00390625
- w_cmat: bfloat16 [2560, 128], replicated, may hold values from -0.125 to 0.125
- conv_inner: float32 [4, 5120], P(None, 'head'), may hold values from -3 to 3
- conv_bc: float32 [4, 256], replicated, may hold values from -3 to 3
- skip_gain: float32 [80], P('head'), may hold values from 0.5 to 2
- w_out: bfloat16 [5120, 2560], P('head'), may hold values from -0.078125 to 0.078125
Outputs:
- output: bfloat16 [4096, 2560], P('ctx', 'head')
- output_tangent: bfloat16 [4096, 2560], P('ctx', 'head')
The draws below stay inside these ranges and needn't reach their ends.
Inputs may be any that keep to these rules, and one draw needn't show every extreme that they name: `log_decay`: negative; the natural logarithm of the factor by which each head's state is multiplied at each token.
All inputs are finite; a program needn't handle non-finite values.
Results may differ from the reference program's by a relative error of at most 0.019.
Values may be sent and summed in bfloat16 or wider, within the bound.
A program may use at most 128 MiB of HBM per device.

```python
import jax
import jax.numpy as jnp
from jax import lax

D = 2560
HEADS = 80
HEAD_DIM = 64
STATE = 128
SPAN = 256
CONV = 4
TOK_DEV = 512
TOKENS = 4096
INNER = 5120
N_HEAD = 4


def draw_log_decay(key, part):
    key = jax.random.fold_in(key, 7)
    subkeys = jax.random.split(key, 7)
    lasting = jax.random.uniform(subkeys[0], (HEADS,)) < 0.3
    slow_rate = jax.random.uniform(subkeys[1], (HEADS,), jnp.float32, 0.1, 0.3) * 2.302585 / TOKENS
    medium_rate = jax.random.uniform(subkeys[2], (HEADS,), jnp.float32, 0.3, 0.7) / TOK_DEV
    decay_rate = jnp.where(lasting, slow_rate, medium_rate)
    blocks = TOKENS // TOK_DEV
    factor = jnp.exp(jax.random.uniform(subkeys[3], (blocks, 1, HEADS), jnp.float32, -0.7, 0.7))
    jitter = jax.random.uniform(subkeys[4], (blocks, TOK_DEV, HEADS), jnp.float32, 0.5, 1.5)
    steady = -(decay_rate[None, None, :] * factor * jitter).reshape(TOKENS, HEADS)
    places = jax.random.randint(subkeys[5], (3,), 0, TOKENS)
    struck = jnp.any(jnp.arange(TOKENS)[:, None] == places[None, :], axis=1)
    dropped = jax.random.uniform(subkeys[6], (TOKENS, HEADS), jnp.float32, 0.2, 0.5)
    return steady + jnp.where(struck[:, None], jnp.log(1.0 - dropped), 0.0)


def levels(stream_key, dims, shards, low, high):
    factor_of, own = 1.0, jax.random.fold_in(stream_key, 6)
    for dim, shards_of in shards:
        draws = jnp.exp(jax.random.uniform(jax.random.fold_in(own, dim), (shards_of,), jnp.float32, low / len(shards), high / len(shards)))
        factor_of = factor_of * jnp.repeat(draws, dims[dim] // shards_of).reshape([-1 if axis == dim else 1 for axis in range(len(dims))])
    return factor_of


def centred(own_key, dims, deviation, most, cuts=(), kind=jnp.bfloat16):
    result = jax.random.normal(own_key, dims, jnp.float32) * deviation
    if len(cuts) > 0:
        result = levels(own_key, dims, cuts, -0.22, 0.18) * result
    return jnp.clip(result, min=-most, max=most).astype(kind)


def setup_inputs(seed: int = 0) -> dict:
    keys = jax.random.split(jax.random.key(seed), 12)
    return {
        "tokens": centred(keys[0], (TOKENS, D), 1.0, 6.0, ((0, 8), (1, 4))),
        "tangent_tokens": centred(keys[1], (TOKENS, D), 1.0, 6.0, ((0, 8), (1, 4))),
        "log_decay": draw_log_decay(jax.random.fold_in(keys[11], 71), 0),
        "tangent_decay": centred(keys[3], (TOKENS, HEADS), 0.016, 0.096, ((0, 8), (1, 4)), jnp.float32),
        "w_inner": centred(keys[4], (D, INNER), D ** -0.5, 0.125, ((1, 4),)),
        "w_bmat": centred(keys[5], (D, STATE), (D * TOKENS * STATE // 512) ** -0.5, 0.00390625),
        "w_cmat": centred(keys[6], (D, STATE), D ** -0.5, 0.125),
        "conv_inner": centred(keys[7], (CONV, INNER), CONV ** -0.5, 3.0, ((1, 4),), jnp.float32),
        "conv_bc": centred(keys[8], (CONV, 2 * STATE), CONV ** -0.5, 3.0, (), jnp.float32),
        "skip_gain": jnp.clip(0.5 + 1.5 * jax.random.uniform(keys[9], (HEADS,), jnp.float32) ** levels(keys[9], (HEADS,), ((0, 4),), -0.2, 0.2), 0.5, 2.0),
        "w_out": centred(keys[10], (INNER, D), INNER ** -0.5, 0.078125, ((0, 4),)),
    }


def depthwise(padded, kernel):
    length = padded.shape[0] - kernel.shape[0] + 1
    summed = kernel[0] * padded[0:length]
    for offset in range(1, kernel.shape[0]):
        summed = summed + kernel[offset] * padded[offset:offset + length]
    return summed


def activate(values):
    return jax.nn.silu(values).astype(jnp.bfloat16)


def span_parts(inputs, writer, reader, decays):
    cumulative = jnp.cumsum(decays, axis=0)
    length = decays.shape[0]
    causal = lax.broadcasted_iota(jnp.int32, (length, length), 0) >= lax.broadcasted_iota(jnp.int32, (length, length), 1)
    differences = cumulative.T[:, :, None] - cumulative.T[:, None, :]
    weights = jnp.exp(jnp.where(causal[None], differences, -jnp.inf))
    scores = jnp.dot(reader, writer.T, preferred_element_type=jnp.float32)
    mixing = (weights * scores[None]).astype(jnp.bfloat16)
    within = jnp.einsum("hts,shp->thp", mixing.astype(jnp.float32), inputs.astype(jnp.float32), precision=lax.Precision.HIGHEST)
    remaining = jnp.exp(cumulative[-1][None, :] - cumulative)
    scaled = (inputs * remaining[:, :, None]).astype(jnp.bfloat16)
    block_state = jnp.einsum("shp,sn->hpn", scaled.astype(jnp.float32), writer.astype(jnp.float32), precision=lax.Precision.HIGHEST)
    return cumulative, within, block_state


def carried(reader, cumulative, initial):
    rounded = initial.astype(jnp.bfloat16)
    readout = jnp.einsum("tn,hpn->thp", reader.astype(jnp.float32), rounded.astype(jnp.float32), precision=lax.Precision.HIGHEST)
    return jnp.exp(cumulative)[:, :, None] * readout


def reference(tokens, tangent_tokens, log_decay, tangent_decay, w_inner, w_bmat, w_cmat, conv_inner, conv_bc, skip_gain, w_out):
    kernel = jnp.concatenate([conv_inner, conv_bc], 1)
    blocks = TOKENS // SPAN

    def sequence_mix(source, decays):
        projected = jnp.concatenate([
            jnp.dot(source, w_inner, preferred_element_type=jnp.float32).astype(jnp.bfloat16),
            jnp.dot(source, w_bmat, preferred_element_type=jnp.float32).astype(jnp.bfloat16),
            jnp.dot(source, w_cmat, preferred_element_type=jnp.float32).astype(jnp.bfloat16)], 1)
        padded = jnp.concatenate([jnp.zeros((CONV - 1, projected.shape[1]), jnp.bfloat16), projected], 0)
        mixed = activate(depthwise(padded, kernel))
        inputs = mixed[:, :INNER].reshape(blocks, SPAN, HEADS, HEAD_DIM)
        writer = mixed[:, INNER:INNER + STATE].reshape(blocks, SPAN, STATE)
        reader = mixed[:, INNER + STATE:].reshape(blocks, SPAN, STATE)
        decay_blocks = decays.reshape(blocks, SPAN, HEADS)

        def advance(initial, block):
            block_inputs, block_writer, block_reader, block_decays = block
            cumulative, within, block_state = span_parts(block_inputs, block_writer, block_reader, block_decays)
            combined = (within + carried(block_reader, cumulative, initial)) + skip_gain[None, :, None] * block_inputs
            following = jnp.exp(cumulative[-1])[:, None, None] * initial + block_state
            return following, combined.astype(jnp.bfloat16)

        start_state = jnp.zeros((HEADS, HEAD_DIM, STATE), jnp.float32)
        finished, outputs = lax.scan(advance, start_state, (inputs, writer, reader, decay_blocks))
        return outputs.reshape(TOKENS, INNER)

    inner, inner_tangent = jax.jvp(sequence_mix, (tokens, log_decay), (tangent_tokens, tangent_decay))
    group = INNER // N_HEAD

    def project(values):
        summed = jnp.zeros((TOKENS, D), jnp.float32)
        for member in range(N_HEAD):
            partial_term = jnp.dot(values[:, member * group:(member + 1) * group], w_out[member * group:(member + 1) * group], preferred_element_type=jnp.float32)
            summed = summed + lax.optimization_barrier(partial_term.astype(jnp.bfloat16)).astype(jnp.float32)
        return summed.astype(jnp.bfloat16)

    return project(inner), project(inner_tangent)
```

```python
import functools

import jax
import jax.numpy as jnp
from jax import lax
from jax.experimental import pallas as pl
from jax.experimental.pallas import tpu as pltpu
from jax.sharding import PartitionSpec as P

HEAD_DIM = 64
SPAN = 256
MESH = pl.DeviceIdType.MESH
HIGHEST = lax.Precision.HIGHEST
VMEM_LIMIT = 56 * 1024 * 1024
F32 = jnp.float32
BF16 = jnp.bfloat16


def remote(src, dst, send, recv, device):
    return pltpu.make_async_remote_copy(
        src_ref=src, dst_ref=dst, send_sem=send, recv_sem=recv, device_id=device, device_id_type=MESH
    )


def greet(devices):
    barrier = pltpu.get_barrier_semaphore()
    for device in devices:
        pl.semaphore_signal(barrier, inc=1, device_id=device, device_id_type=MESH)
    pl.semaphore_wait(barrier, len(devices))


def lanes(start, size):
    return pl.ds(pl.multiple_of(start, 128), size)


def gather_project_kernel(
    tok, tan, w_in, w_b, w_c, out,
    held, acc, weight, w_sem, sib_send, sib_recv, far_send, far_recv, fwd_send, fwd_recv,
):
    me = lax.axis_index("head")
    sib = me + 1 - 2 * lax.rem(me, 2)
    far = lax.rem(me + 2, 4)
    far_sib = lax.rem(sib + 2, 4)
    rows_in, feat = tok.shape
    width = w_in.shape[1]
    state = w_b.shape[1]
    chunk = SPAN
    per = rows_in // chunk
    count = 2 * per
    loads = [
        pltpu.make_async_copy(w_in, weight.at[:, 0:width], w_sem.at[0]),
        pltpu.make_async_copy(w_b, weight.at[:, width : width + state], w_sem.at[1]),
        pltpu.make_async_copy(w_c, weight.at[:, width + state : width + 2 * state], w_sem.at[2]),
    ]
    for load in loads:
        load.start()
    greet([{"head": sib}, {"head": far}])

    def own(r):
        ref, at = (tok, r) if r < per else (tan, r - per)
        return ref.at[at * chunk : (at + 1) * chunk]

    def span(r):
        return slice(r * chunk, (r + 1) * chunk)

    far_copies = [
        remote(own(r), held.at[1, span(r)], far_send.at[r], far_recv.at[r], {"head": far})
        for r in range(count)
    ]
    sib_copies = [
        remote(own(r), held.at[0, span(r)], sib_send.at[r], sib_recv.at[r], {"head": sib})
        for r in range(count)
    ]
    fwd_copies = [
        remote(held.at[1, span(r)], held.at[2, span(r)], fwd_send.at[r], fwd_recv.at[r], {"head": sib})
        for r in range(count)
    ]
    for r in range(count):
        far_copies[r].start()
        sib_copies[r].start()
    for load in loads:
        load.wait()
    tiles = weight.shape[1] // 256

    def block(index):
        return pl.ds(pl.multiple_of(index * feat, 128), feat)

    for r in range(count):
        sib_copies[r].wait_recv()

        def near(j, _, r=r):
            cols = lanes(j * 256, 256)
            acc[span(r), cols] = jnp.dot(
                own(r)[...], weight[block(me), cols], preferred_element_type=F32
            ) + jnp.dot(held[0, span(r), :], weight[block(sib), cols], preferred_element_type=F32)
            return 0

        lax.fori_loop(0, tiles, near, 0)

    def finish(r):
        fwd_copies[r].wait_recv()

        def last(j, _):
            cols = lanes(j * 256, 256)
            total = acc[span(r), cols] + jnp.dot(
                held[2, span(r), :], weight[block(far_sib), cols], preferred_element_type=F32
            )
            out[span(r), cols] = total.astype(BF16)
            return 0

        lax.fori_loop(0, tiles, last, 0)

    for r in range(count):
        far_copies[r].wait_recv()
        fwd_copies[r].start()

        def middle(j, _, r=r):
            cols = lanes(j * 256, 256)
            acc[span(r), cols] += jnp.dot(
                held[1, span(r), :], weight[block(far), cols], preferred_element_type=F32
            )
            return 0

        lax.fori_loop(0, tiles, middle, 0)
        if r > 0:
            finish(r - 1)
    finish(count - 1)
    for r in range(count):
        far_copies[r].wait_send()
        sib_copies[r].wait_send()
        fwd_copies[r].wait_send()


def gather_project(tokens, tangent_tokens, w_inner, w_bmat, w_cmat):
    length, feat = tokens.shape
    depth = w_inner.shape[0]
    total = w_inner.shape[1] + 2 * w_bmat.shape[1]
    count = 2 * length // SPAN
    vmem = pl.BlockSpec(memory_space=pltpu.VMEM)
    anywhere = pl.BlockSpec(memory_space=pl.ANY)
    dma = pltpu.SemaphoreType.DMA
    return pl.pallas_call(
        gather_project_kernel,
        out_shape=jax.ShapeDtypeStruct((2 * length, total), BF16),
        in_specs=[vmem, vmem, anywhere, anywhere, anywhere],
        out_specs=vmem,
        scratch_shapes=[
            pltpu.VMEM((3, 2 * length, feat), BF16),
            pltpu.VMEM((2 * length, total), F32),
            pltpu.VMEM((depth, total), BF16),
            dma((3,)),
        ]
        + [dma((count,))] * 6,
        compiler_params=pltpu.CompilerParams(
            collective_id=0, has_side_effects=True, vmem_limit_bytes=VMEM_LIMIT
        ),
        name="gather_project",
    )(tokens, tangent_tokens, w_inner, w_bmat, w_cmat)


def project_scatter_kernel(
    inner, w_out, out, out_dot,
    w_far, w_near, p_far, p_near, r_far, s_far, r_x, r_near,
    w_sem, a_send, a_recv, x_send, x_recv, b_send, b_recv,
):
    me = lax.axis_index("head")
    core = lax.rem(me, 2)
    chip = (me - core) // 2
    sib = me + 1 - 2 * core
    far = lax.rem(me + 2, 4)
    rows = inner.shape[0]
    half = w_far.shape[1]
    feat = half // 2
    count = rows // SPAN
    per = count // 2
    load_far = pltpu.make_async_copy(w_out.at[:, lanes((1 - chip) * half, half)], w_far, w_sem.at[0])
    load_near = pltpu.make_async_copy(w_out.at[:, lanes(chip * half, half)], w_near, w_sem.at[1])
    load_far.start()
    load_near.start()
    greet([{"head": sib}, {"head": far}])
    keep = lanes(core * feat, feat)
    give = lanes((1 - core) * feat, feat)
    tiles = half // 256

    def multiply(r, weight, into):
        def one(j, _):
            cols = lanes(j * 256, 256)
            into[r, :, cols] = jnp.dot(
                inner[r * SPAN : (r + 1) * SPAN, :], weight[:, cols], preferred_element_type=F32
            ).astype(BF16)
            return 0

        lax.fori_loop(0, tiles, one, 0)

    a_copies = [
        remote(p_far.at[r, :, give], r_far.at[r], a_send.at[r], a_recv.at[r], {"head": sib})
        for r in range(count)
    ]
    x_copies = [
        remote(s_far.at[r], r_x.at[r], x_send.at[r], x_recv.at[r], {"head": far})
        for r in range(count)
    ]
    b_copies = [
        remote(p_near.at[r, :, give], r_near.at[r], b_send.at[r], b_recv.at[r], {"head": sib})
        for r in range(count)
    ]

    def pass_on(r):
        a_copies[r].wait_recv()
        s_far[r] = (p_far[r, :, keep].astype(F32) + r_far[r].astype(F32)).astype(BF16)
        x_copies[r].start()

    load_far.wait()
    for r in range(count):
        multiply(r, w_far, p_far)
        a_copies[r].start()
        if r > 0:
            pass_on(r - 1)
    load_near.wait()
    for r in range(count):
        multiply(r, w_near, p_near)
        b_copies[r].start()
        if r == 0:
            pass_on(count - 1)
    for r in range(count):
        b_copies[r].wait_recv()
        x_copies[r].wait_recv()
        total = p_near[r, :, keep].astype(F32) + r_near[r].astype(F32) + r_x[r].astype(F32)
        ref, at = (out, r) if r < per else (out_dot, r - per)
        ref[at * SPAN : (at + 1) * SPAN, :] = total.astype(BF16)
    for r in range(count):
        a_copies[r].wait_send()
        b_copies[r].wait_send()
        x_copies[r].wait_send()


def project_scatter(inner, w_out):
    rows, width = inner.shape
    full = w_out.shape[1]
    half, feat = full // 2, full // 4
    count = rows // SPAN
    vmem = pl.BlockSpec(memory_space=pltpu.VMEM)
    dma = pltpu.SemaphoreType.DMA
    result = jax.ShapeDtypeStruct((rows // 2, feat), BF16)
    return pl.pallas_call(
        project_scatter_kernel,
        out_shape=(result, result),
        in_specs=[vmem, pl.BlockSpec(memory_space=pl.ANY)],
        out_specs=(vmem, vmem),
        scratch_shapes=[
            pltpu.VMEM((width, half), BF16),
            pltpu.VMEM((width, half), BF16),
            pltpu.VMEM((count, SPAN, half), BF16),
            pltpu.VMEM((count, SPAN, half), BF16),
        ]
        + [pltpu.VMEM((count, SPAN, feat), BF16)] * 4
        + [dma((2,))]
        + [dma((count,))] * 6,
        compiler_params=pltpu.CompilerParams(
            collective_id=2, has_side_effects=True, vmem_limit_bytes=VMEM_LIMIT
        ),
        name="project_scatter",
    )(inner, w_out)


def mix_kernel(
    proj, decay, decay_dot, conv_in, conv_bc, skip, out,
    halo, padded, pad_dec, cum, cum_dot, cum_t, cum_dot_t, wide, wide_dot, x, x_dot, bc, bc_dot,
    score, score_dot, within, within_dot, state, state_dot,
    total, rows, pair_total, pair_rows, chain_in, chain_out, give, entry,
    halo_send, halo_recv, pair_send, pair_recv, chain_send, chain_recv, give_send, give_recv,
):
    me = lax.axis_index("ctx")
    count = lax.axis_size("ctx")
    odd = lax.rem(me, 2)
    partner = me + 1 - 2 * odd
    length = proj.shape[0] // 2
    width = x.shape[1]
    heads = decay.shape[1]
    pairs = width // 128
    half = pairs // 2
    blocks = length // SPAN
    state_len = bc.shape[1] // 2
    lane = lax.broadcasted_iota(jnp.int32, (1, 128), 1)

    barrier = pltpu.get_barrier_semaphore()
    for step in (-2, -1, 1, 2):
        other = me + step

        @pl.when(jnp.logical_and(other >= 0, other < count))
        def _(other=other):
            pl.semaphore_signal(barrier, inc=1, device_id={"ctx": other}, device_id_type=MESH)

    pl.semaphore_wait(barrier, jnp.minimum(me, 2) + jnp.minimum(count - 1 - me, 2))

    halo_copies = [
        remote(
            proj.at[(k + 1) * length - 16 : (k + 1) * length, :],
            halo.at[k],
            halo_send.at[k],
            halo_recv.at[k],
            {"ctx": me + 1},
        )
        for k in range(2)
    ]

    @pl.when(me + 1 < count)
    def _():
        for copy in halo_copies:
            copy.start()

    @pl.when(me < 2)
    def _():
        chain_in[...] = jnp.zeros_like(chain_in)

    pad_dec[...] = jnp.zeros_like(pad_dec)
    pad_dec[0, :, 0:heads] = decay[...]
    pad_dec[1, :, 0:heads] = decay_dot[...]
    t_index = lax.broadcasted_iota(jnp.int32, (SPAN, SPAN), 0)
    s_index = lax.broadcasted_iota(jnp.int32, (SPAN, SPAN), 1)
    lower = (t_index >= s_index).astype(F32)
    for b in range(blocks):
        at = slice(b * SPAN, (b + 1) * SPAN)
        for source, into, into_t in ((0, cum, cum_t), (1, cum_dot, cum_dot_t)):
            summed = jnp.dot(lower, pad_dec[source, at, :], precision=HIGHEST, preferred_element_type=F32)
            into[at, :] = summed
            into_t[b] = summed.T
    cum[length : length + 8, :] = jnp.zeros((8, 128), F32)
    cum[length : length + 1, 0:heads] = skip[...]

    def expand(p, _):
        cols = lanes(p * 128, 128)
        source = lax.broadcasted_iota(jnp.int32, (128, 128), 0)
        target = lax.broadcasted_iota(jnp.int32, (128, 128), 1)
        pick = (source == 2 * p + (target >= HEAD_DIM).astype(jnp.int32)).astype(F32)
        wide[:, cols] = jnp.dot(cum[...], pick, precision=HIGHEST, preferred_element_type=F32)
        wide_dot[:, cols] = jnp.dot(cum_dot[...], pick, precision=HIGHEST, preferred_element_type=F32)
        return 0

    lax.fori_loop(0, pairs, expand, 0)

    @pl.when(me == 0)
    def _():
        halo[...] = jnp.zeros_like(halo)

    @pl.when(me > 0)
    def _():
        for copy in halo_copies:
            copy.wait_recv()

    def convolve(cols, kernel, into, into_dot, to):
        for b in range(blocks):
            start = b * SPAN
            convs = []
            for k in range(2):
                if b == 0:
                    padded[k, 0:16, :] = halo[k, :, cols].astype(F32)
                else:
                    padded[k, 0:16, :] = proj[k * length + start - 16 : k * length + start, cols].astype(F32)
                padded[k, 16 : 16 + SPAN, :] = proj[k * length + start : k * length + start + SPAN, cols].astype(F32)
                summed = kernel[0:1, :] * padded[k, 13 : 13 + SPAN, :]
                for tap in range(1, 4):
                    summed = summed + kernel[tap : tap + 1, :] * padded[k, 13 + tap : 13 + tap + SPAN, :]
                convs.append(summed)
            gate = 1.0 / (1.0 + jnp.exp(-convs[0]))
            into[start : start + SPAN, to] = (convs[0] * gate).astype(BF16)
            into_dot[start : start + SPAN, to] = (
                convs[1] * (gate * (1.0 + convs[0] * (1.0 - gate)))
            ).astype(BF16)

    for k in range(2):
        span = slice(k * state_len, (k + 1) * state_len)
        convolve(
            slice(width + k * state_len, width + (k + 1) * state_len), conv_bc[:, span], bc, bc_dot, span
        )

    def convolve_inner(p, _):
        cols = lanes(p * 128, 128)
        convolve(cols, conv_in[:, cols], x, x_dot, cols)
        return 0

    lax.fori_loop(0, pairs, convolve_inner, 0)

    writer_t = [bc[b * SPAN : (b + 1) * SPAN, 0:state_len].T for b in range(blocks)]
    writer_dot_t = [bc_dot[b * SPAN : (b + 1) * SPAN, 0:state_len].T for b in range(blocks)]

    def states(p, _):
        cols = lanes(p * 128, 128)
        sums = None
        for b in range(blocks):
            at = slice(b * SPAN, (b + 1) * SPAN)
            end = slice((b + 1) * SPAN - 1, (b + 1) * SPAN)
            last, last_dot = wide[end, cols], wide_dot[end, cols]
            remaining = jnp.exp(last - wide[at, cols])
            values = x[at, cols].astype(F32)
            scaled = (values * remaining).astype(BF16)
            scaled_dot = (
                (x_dot[at, cols].astype(F32) + values * (last_dot - wide_dot[at, cols])) * remaining
            ).astype(BF16)
            new = jnp.dot(writer_t[b], scaled, preferred_element_type=F32)
            new_dot = jnp.dot(writer_t[b], scaled_dot, preferred_element_type=F32) + jnp.dot(
                writer_dot_t[b], scaled, preferred_element_type=F32
            )
            state[b, :, cols] = new
            state_dot[b, :, cols] = new_dot
            if sums is None:
                sums = (last, last_dot, new, new_dot)
            else:
                log, slope, old, old_dot = sums
                retain = jnp.exp(last)
                sums = (
                    log + last,
                    slope + last_dot,
                    retain * old + new,
                    retain * (old_dot + last_dot * old) + new_dot,
                )
        log, slope, old, old_dot = sums
        rows[p] = jnp.concatenate([log, slope, jnp.zeros((6, 128), F32)], 0)
        total[p, 0] = old.astype(BF16)
        total[p, 1] = old_dot.astype(BF16)
        return 0

    lax.fori_loop(0, pairs, states, 0)

    mine = odd * half
    others = (1 - odd) * half
    pair_copies = [
        remote(total.at[pl.ds(others, half)], pair_total, pair_send.at[0], pair_recv.at[0], {"ctx": partner}),
        remote(rows.at[pl.ds(others, half)], pair_rows, pair_send.at[1], pair_recv.at[1], {"ctx": partner}),
    ]
    for copy in pair_copies:
        copy.start()

    def outer_t(left, right):
        return lax.dot_general(left, right, (((1,), (1,)), ((), ())), preferred_element_type=F32)

    for b in range(blocks):
        at = slice(b * SPAN, (b + 1) * SPAN)
        writer, reader = bc[at, 0:state_len], bc[at, state_len : 2 * state_len]
        writer_dot, reader_dot = bc_dot[at, 0:state_len], bc_dot[at, state_len : 2 * state_len]
        causal = t_index >= s_index
        score[b] = jnp.where(causal, outer_t(reader, writer), 0.0)
        score_dot[b] = jnp.where(causal, outer_t(reader_dot, writer) + outer_t(reader, writer_dot), 0.0)

    def mixing(p, _):
        cols = lanes(p * 128, 128)
        for b in range(blocks):
            for t in range(SPAN // 128):
                size = (t + 1) * 128
                at = slice(b * SPAN + t * 128, b * SPAN + size)
                upto = slice(b * SPAN, b * SPAN + size)
                tile = slice(t * 128, size)
                values = x[upto, cols]
                both = jnp.concatenate([values, x_dot[upto, cols]], 1)
                column, column_dot = wide[at, cols], wide_dot[at, cols]
                found = []
                for k in range(2):
                    first = k * HEAD_DIM
                    row = cum_t[b, pl.ds(2 * p + k, 1), :][:, 0:size]
                    row_dot = cum_dot_t[b, pl.ds(2 * p + k, 1), :][:, 0:size]
                    weight = jnp.exp(jnp.minimum(column[:, first : first + 1] - row, 0.0))
                    change = column_dot[:, first : first + 1] - row_dot
                    scores = score[b, tile, 0:size]
                    mix = (weight * scores).astype(BF16)
                    mix_dot = (weight * (score_dot[b, tile, 0:size] + change * scores)).astype(BF16)
                    found.append(
                        (
                            jnp.dot(mix, both, preferred_element_type=F32),
                            jnp.dot(mix_dot, values, preferred_element_type=F32),
                        )
                    )
                (r0, q0), (r1, q1) = found
                within[at, cols] = jnp.where(lane < HEAD_DIM, r0[:, 0:128], r1[:, 0:128])
                within_dot[at, cols] = jnp.where(lane < HEAD_DIM, r0[:, 128:256] + q0, r1[:, 128:256] + q1)
        return 0

    lax.fori_loop(0, pairs, mixing, 0)

    for copy in pair_copies:
        copy.wait_recv()

    chain_copies = [
        remote(chain_out.at[i], chain_in.at[i], chain_send.at[i], chain_recv.at[i], {"ctx": me + 2})
        for i in range(half)
    ]
    give_copies = [
        remote(give.at[i], entry.at[mine + i], give_send.at[i], give_recv.at[i], {"ctx": partner})
        for i in range(half)
    ]
    first_here = odd == 0
    for i in range(half):

        @pl.when(me >= 2)
        def _(i=i):
            chain_copies[i].wait_recv()

        arrived, arrived_dot = chain_in[i, 0].astype(F32), chain_in[i, 1].astype(F32)
        own, own_dot = total[mine + i, 0].astype(F32), total[mine + i, 1].astype(F32)
        their, their_dot = pair_total[i, 0].astype(F32), pair_total[i, 1].astype(F32)
        own_rows, their_rows = rows[mine + i], pair_rows[i]
        early_rows = jnp.where(first_here, own_rows, their_rows)
        late_rows = jnp.where(first_here, their_rows, own_rows)
        retain = jnp.exp(early_rows[0:1])
        middle = retain * arrived + jnp.where(first_here, own, their)
        middle_dot = retain * (arrived_dot + early_rows[1:2] * arrived) + jnp.where(
            first_here, own_dot, their_dot
        )
        retain = jnp.exp(late_rows[0:1])
        chain_out[i, 0] = (retain * middle + jnp.where(first_here, their, own)).astype(BF16)
        chain_out[i, 1] = (
            retain * (middle_dot + late_rows[1:2] * middle) + jnp.where(first_here, their_dot, own_dot)
        ).astype(BF16)

        @pl.when(me + 2 < count)
        def _(i=i):
            chain_copies[i].start()

        give[i, 0] = jnp.where(first_here, middle, arrived).astype(BF16)
        give[i, 1] = jnp.where(first_here, middle_dot, arrived_dot).astype(BF16)
        give_copies[i].start()
        entry[mine + i, 0] = jnp.where(first_here, arrived, middle).astype(BF16)
        entry[mine + i, 1] = jnp.where(first_here, arrived_dot, middle_dot).astype(BF16)

    def finish(p, _):
        cols = lanes(p * 128, 128)
        gain = wide[length : length + 1, cols]
        now, now_dot = entry[p, 0], entry[p, 1]
        for b in range(blocks):
            at = slice(b * SPAN, (b + 1) * SPAN)
            end = slice((b + 1) * SPAN - 1, (b + 1) * SPAN)
            reader = bc[at, state_len : 2 * state_len]
            reader_dot = bc_dot[at, state_len : 2 * state_len]
            read = jnp.dot(reader, jnp.concatenate([now, now_dot], 1), preferred_element_type=F32)
            moved = jnp.dot(reader_dot, now, preferred_element_type=F32)
            grown = jnp.exp(wide[at, cols])
            plain = read[:, 0:128]
            out[at, cols] = (
                within[at, cols] + grown * plain + gain * x[at, cols].astype(F32)
            ).astype(BF16)
            out[length + b * SPAN : length + (b + 1) * SPAN, cols] = (
                within_dot[at, cols]
                + grown * (read[:, 128:256] + moved + wide_dot[at, cols] * plain)
                + gain * x_dot[at, cols].astype(F32)
            ).astype(BF16)
            if b + 1 < blocks:
                retain = jnp.exp(wide[end, cols])
                old, old_dot = now.astype(F32), now_dot.astype(F32)
                now = (retain * old + state[b, :, cols]).astype(BF16)
                now_dot = (
                    retain * (old_dot + wide_dot[end, cols] * old) + state_dot[b, :, cols]
                ).astype(BF16)
        return 0

    lax.fori_loop(mine, mine + half, finish, 0)
    back_copies = [
        remote(give.at[i], entry.at[others + i], give_send.at[i], give_recv.at[i], {"ctx": partner})
        for i in range(half)
    ]
    for i in range(half):
        back_copies[i].wait_recv()
    lax.fori_loop(others, others + half, finish, 0)

    for copy in pair_copies + give_copies:
        copy.wait_send()

    @pl.when(me + 1 < count)
    def _():
        for copy in halo_copies:
            copy.wait_send()

    @pl.when(me + 2 < count)
    def _():
        for copy in chain_copies:
            copy.wait_send()


def mix(projected, log_decay, tangent_decay, conv_inner, conv_bc, skip_gain):
    length = log_decay.shape[0]
    width = conv_inner.shape[1]
    state_len = conv_bc.shape[1] // 2
    blocks = length // SPAN
    pairs = width // 128
    half = pairs // 2
    vmem = pl.BlockSpec(memory_space=pltpu.VMEM)
    dma = pltpu.SemaphoreType.DMA
    piece = (2, state_len, 128)
    return pl.pallas_call(
        mix_kernel,
        out_shape=jax.ShapeDtypeStruct((2 * length, width), BF16),
        in_specs=[vmem] * 6,
        out_specs=vmem,
        scratch_shapes=[
            pltpu.VMEM((2, 16, width + 2 * state_len), BF16),
            pltpu.VMEM((2, 16 + SPAN, 128), F32),
            pltpu.VMEM((2, length, 128), F32),
            pltpu.VMEM((length + 8, 128), F32),
            pltpu.VMEM((length, 128), F32),
            pltpu.VMEM((blocks, 128, SPAN), F32),
            pltpu.VMEM((blocks, 128, SPAN), F32),
            pltpu.VMEM((length + 8, width), F32),
            pltpu.VMEM((length, width), F32),
            pltpu.VMEM((length, width), BF16),
            pltpu.VMEM((length, width), BF16),
            pltpu.VMEM((length, 2 * state_len), BF16),
            pltpu.VMEM((length, 2 * state_len), BF16),
            pltpu.VMEM((blocks, SPAN, SPAN), F32),
            pltpu.VMEM((blocks, SPAN, SPAN), F32),
            pltpu.VMEM((length, width), F32),
            pltpu.VMEM((length, width), F32),
            pltpu.VMEM((blocks, state_len, width), F32),
            pltpu.VMEM((blocks, state_len, width), F32),
            pltpu.VMEM((pairs, *piece), BF16),
            pltpu.VMEM((pairs, 8, 128), F32),
            pltpu.VMEM((half, *piece), BF16),
            pltpu.VMEM((half, 8, 128), F32),
            pltpu.VMEM((half, *piece), BF16),
            pltpu.VMEM((half, *piece), BF16),
            pltpu.VMEM((half, *piece), BF16),
            pltpu.VMEM((pairs, *piece), BF16),
            dma((2,)),
            dma((2,)),
            dma((2,)),
            dma((2,)),
            dma((half,)),
            dma((half,)),
            dma((half,)),
            dma((half,)),
        ],
        compiler_params=pltpu.CompilerParams(
            collective_id=1, has_side_effects=True, vmem_limit_bytes=VMEM_LIMIT
        ),
        name="mix",
    )(projected, log_decay, tangent_decay, conv_inner, conv_bc, skip_gain.reshape(1, -1))


def fused_on_device(
    tokens, tangent_tokens, log_decay, tangent_decay, w_inner, w_bmat, w_cmat,
    conv_inner, conv_bc, skip_gain, w_out,
):
    projected = gather_project(tokens, tangent_tokens, w_inner, w_bmat, w_cmat)
    inner = mix(projected, log_decay, tangent_decay, conv_inner, conv_bc, skip_gain)
    return project_scatter(inner, w_out)


def shifted(block, axis, distance):
    devices = range(lax.axis_size(axis))
    route = [(i - distance, i) for i in devices if i - distance in devices]
    return lax.ppermute(block, axis, route)


def carried_in(part, axis, combine, identity):
    place = lax.axis_index(axis)
    gathered = jax.tree.map(lambda a: lax.all_gather(a, axis), part)
    state = jax.tree.map(lambda a, e: jnp.zeros_like(a) + jnp.asarray(e, a.dtype), part, identity)

    def one(step, state):
        return combine(
            state, jax.tree.map(lambda a: lax.dynamic_index_in_dim(a, step, 0, False), gathered)
        )

    return lax.fori_loop(0, place, one, state)


def depthwise(padded, kernel):
    length = padded.shape[0] - kernel.shape[0] + 1
    summed = kernel[0] * padded[0:length]
    for offset in range(1, kernel.shape[0]):
        summed = summed + kernel[offset] * padded[offset : offset + length]
    return summed


def activate(values):
    return jax.nn.silu(values).astype(jnp.bfloat16)


def span_parts(inputs, writer, reader, decays):
    cumulative = jnp.cumsum(decays, axis=0)
    length = decays.shape[0]
    causal = lax.broadcasted_iota(jnp.int32, (length, length), 0) >= lax.broadcasted_iota(
        jnp.int32, (length, length), 1
    )
    differences = cumulative.T[:, :, None] - cumulative.T[:, None, :]
    weights = jnp.exp(jnp.where(causal[None], differences, -jnp.inf))
    scores = jnp.dot(reader, writer.T, preferred_element_type=jnp.float32)
    mixing = (weights * scores[None]).astype(jnp.bfloat16)
    within = jnp.einsum("hts,shp->thp", mixing, inputs, preferred_element_type=jnp.float32)
    remaining = jnp.exp(cumulative[-1][None, :] - cumulative)
    scaled = (inputs * remaining[:, :, None]).astype(jnp.bfloat16)
    block_state = jnp.einsum("shp,sn->hpn", scaled, writer, preferred_element_type=jnp.float32)
    return (cumulative, within, block_state)


def carried(reader, cumulative, initial):
    readout = jnp.einsum(
        "tn,hpn->thp", reader, initial.astype(jnp.bfloat16), preferred_element_type=jnp.float32
    )
    return jnp.exp(cumulative)[:, :, None] * readout


def combine(earlier, later):
    early_total, early_slope, early_state, early_tangent = earlier
    late_total, late_slope, late_state, late_tangent = later
    retain = jnp.exp(late_total)
    return (
        early_total + late_total,
        early_slope + late_slope,
        retain * early_state + late_state,
        retain * (early_tangent + late_slope * early_state) + late_tangent,
    )


def on_device(
    tokens,
    tangent_tokens,
    log_decay,
    tangent_decay,
    w_inner,
    w_bmat,
    w_cmat,
    conv_inner,
    conv_bc,
    skip_gain,
    w_out,
):
    length = tokens.shape[0]
    width = w_inner.shape[1]
    state_len = w_bmat.shape[1]
    heads_here = width // HEAD_DIM
    margin = conv_inner.shape[0] - 1
    blocks = length // SPAN
    stacked = jnp.concatenate([tokens, tangent_tokens], 0)
    shard_piece = lax.all_gather(stacked, "head", axis=1, tiled=True)
    sums = (
        jnp.dot(shard_piece, w_inner, preferred_element_type=jnp.float32),
        jnp.dot(shard_piece, w_bmat, preferred_element_type=jnp.float32),
        jnp.dot(shard_piece, w_cmat, preferred_element_type=jnp.float32),
    )
    projected = jnp.concatenate([summand.astype(jnp.bfloat16) for summand in sums], 1)
    edges = jnp.stack([projected[length - margin : length], projected[2 * length - margin :]])
    previous = shifted(edges, "ctx", 1)
    kernel = jnp.concatenate([conv_inner, conv_bc], 1)
    primal_conv = depthwise(jnp.concatenate([previous[0], projected[:length]], 0), kernel)
    tangent_conv = depthwise(jnp.concatenate([previous[1], projected[length:]], 0), kernel)
    mixed, mixed_dot = jax.jvp(activate, (primal_conv,), (tangent_conv,))

    def separate(values):
        inputs = values[:, :width].reshape(blocks, SPAN, heads_here, HEAD_DIM)
        writer = values[:, width : width + state_len].reshape(blocks, SPAN, state_len)
        reader = values[:, width + state_len :].reshape(blocks, SPAN, state_len)
        return (inputs, writer, reader)

    inputs, writer, reader = separate(mixed)
    inputs_dot, writer_dot, reader_dot = separate(mixed_dot)
    decays = log_decay.reshape(blocks, SPAN, heads_here)
    decays_dot = tangent_decay.reshape(blocks, SPAN, heads_here)
    (cumulative, within, block_state), (cumulative_dot, within_dot, block_dot) = jax.jvp(
        jax.vmap(span_parts),
        (inputs, writer, reader, decays),
        (inputs_dot, writer_dot, reader_dot, decays_dot),
    )

    def summarize(cumulative, block_state):
        summed = cumulative[0, -1]
        running = block_state[0]
        summed = summed + cumulative[1, -1]
        running = jnp.exp(cumulative[1, -1])[:, None, None] * running + block_state[1]
        return (summed[:, None, None], running)

    (decay_sum, own_state), (decay_sum_dot, own_dot) = jax.jvp(
        summarize, (cumulative, block_state), (cumulative_dot, block_dot)
    )
    message = (decay_sum, decay_sum_dot, own_state, own_dot)
    empty = tuple((jnp.zeros_like(member) for member in message))
    arriving = carried_in(message, "ctx", combine, empty)
    entry_state = arriving[2]
    entry_dot = arriving[3]

    def finish(initial, cumulative, within, block_state, inputs, reader):
        outputs = []
        for position in range(cumulative.shape[0]):
            combined = (
                within[position]
                + carried(reader[position], cumulative[position], initial)
                + skip_gain[None, :, None] * inputs[position]
            )
            outputs.append(combined.astype(jnp.bfloat16))
            if position + 1 < cumulative.shape[0]:
                initial = (
                    jnp.exp(cumulative[position, -1])[:, None, None] * initial
                    + block_state[position]
                )
        return jnp.stack(outputs)

    inner, inner_dot = jax.jvp(
        finish,
        (entry_state, cumulative, within, block_state, inputs, reader),
        (entry_dot, cumulative_dot, within_dot, block_dot, inputs_dot, reader_dot),
    )
    flattened = jnp.concatenate([inner.reshape(length, width), inner_dot.reshape(length, width)], 0)
    partial_term = jnp.dot(flattened, w_out, preferred_element_type=jnp.float32).astype(
        jnp.bfloat16
    )
    summed = (
        lax.psum_scatter(partial_term, "head", scatter_dimension=1, tiled=True)
        .astype(jnp.float32)
        .astype(jnp.bfloat16)
    )
    return (summed[:length], summed[length:])


def solution(mesh):
    in_specs = (
        P("ctx", "head"),
        P("ctx", "head"),
        P("ctx", "head"),
        P("ctx", "head"),
        P(None, "head"),
        P(),
        P(),
        P(None, "head"),
        P(),
        P("head"),
        P("head", None),
    )
    out_specs = (P("ctx", "head"), P("ctx", "head"))
    fits = mesh.shape["head"] == 4 and mesh.shape["ctx"] % 2 == 0
    return jax.shard_map(
        fused_on_device if fits else on_device, mesh=mesh, in_specs=in_specs, out_specs=out_specs, check_vma=False
    )
```

```python
import functools

import jax
import jax.numpy as jnp
from jax import lax
from jax.experimental import pallas as pl
from jax.experimental.pallas import tpu as pltpu
from jax.sharding import PartitionSpec as P

HEAD_DIM = 64
SPAN = 256
MESH = pl.DeviceIdType.MESH
HIGHEST = lax.Precision.HIGHEST
VMEM_LIMIT = 60 * 1024 * 1024
F32 = jnp.float32
BF16 = jnp.bfloat16


def remote(src, dst, send, recv, device):
    return pltpu.make_async_remote_copy(
        src_ref=src, dst_ref=dst, send_sem=send, recv_sem=recv, device_id=device, device_id_type=MESH
    )


def lanes(start, size):
    return pl.ds(pl.multiple_of(start, 128), size)


def layer_kernel(
    tok, tan, decay_t, decay_dot_t, w_in, w_b, w_c, conv_in, conv_bc, skip, w_out, out, out_dot,
    held, acc, weight, proj, inner,
    halo, padded, pad_dec, cum, cum_dot, cum_t, cum_dot_t, wide, wide_dot, x, x_dot, bc, bc_dot,
    score, score_dot, within, within_dot, state, state_dot,
    total, rows, pair_total, pair_rows, chain_in, chain_out, give, entry,
    p_near, r_far, s_far, r_x, r_near,
    w_sem, sib_send, sib_recv, far_send, far_recv, fwd_send, fwd_recv,
    halo_send, halo_recv, pair_send, pair_recv, chain_send, chain_recv, give_send, give_recv,
    a_send, a_recv, x_send, x_recv, b_send, b_recv,
):
    head = lax.axis_index("head")
    core = lax.rem(head, 2)
    chip = (head - core) // 2
    sib = head + 1 - 2 * core
    far = lax.rem(head + 2, 4)
    far_sib = lax.rem(sib + 2, 4)
    me = lax.axis_index("ctx")
    count = lax.axis_size("ctx")
    odd = lax.rem(me, 2)
    partner = me + 1 - 2 * odd
    length, feat = tok.shape
    width = x.shape[1]
    heads = decay_t.shape[0]
    pairs = width // 128
    half = pairs // 2
    blocks = length // SPAN
    state_len = bc.shape[1] // 2
    lane = lax.broadcasted_iota(jnp.int32, (1, 128), 1)

    loads = [
        pltpu.make_async_copy(w_in, weight.at[:, 0:width], w_sem.at[0]),
        pltpu.make_async_copy(w_b, weight.at[:, width : width + state_len], w_sem.at[1]),
        pltpu.make_async_copy(w_c, weight.at[:, width + state_len :], w_sem.at[2]),
    ]
    for load in loads:
        load.start()

    barrier = pltpu.get_barrier_semaphore()
    for other in (sib, far):
        pl.semaphore_signal(barrier, inc=1, device_id={"head": other}, device_id_type=MESH)
    for step in (-2, -1, 1, 2):
        other = me + step

        @pl.when(jnp.logical_and(other >= 0, other < count))
        def _(other=other):
            pl.semaphore_signal(barrier, inc=1, device_id={"ctx": other}, device_id_type=MESH)

    pl.semaphore_wait(barrier, 2 + jnp.minimum(me, 2) + jnp.minimum(count - 1 - me, 2))

    cut = length - SPAN - 16
    chunks = [(0, cut, length - cut), (1, cut, length - cut), (0, 0, cut), (1, 0, cut)]

    def own(c):
        k, start, size = chunks[c]
        return (tok, tan)[k].at[start : start + size]

    def span(c):
        k, start, size = chunks[c]
        return slice(k * length + start, k * length + start + size)

    order = range(len(chunks))
    far_copies = [
        remote(own(c), held.at[1, span(c)], far_send.at[c], far_recv.at[c], {"head": far}) for c in order
    ]
    sib_copies = [
        remote(own(c), held.at[0, span(c)], sib_send.at[c], sib_recv.at[c], {"head": sib}) for c in order
    ]
    fwd_copies = [
        remote(held.at[1, span(c)], held.at[2, span(c)], fwd_send.at[c], fwd_recv.at[c], {"head": sib})
        for c in order
    ]
    for c in order:
        far_copies[c].start()
        sib_copies[c].start()
    tiles = weight.shape[1] // 256

    def block(index):
        return pl.ds(pl.multiple_of(index * feat, 128), feat)

    def near(c):
        sib_copies[c].wait_recv()
        size = chunks[c][2]

        def one(j, _):
            cols = lanes(j * 256, 256)
            acc[0:size, cols] = jnp.dot(
                own(c)[...], weight[block(head), cols], preferred_element_type=F32
            ) + jnp.dot(held[0, span(c), :], weight[block(sib), cols], preferred_element_type=F32)
            return 0

        lax.fori_loop(0, tiles, one, 0)

    def forward(c):
        far_copies[c].wait_recv()
        fwd_copies[c].start()

    def distant(c):
        size = chunks[c][2]

        def middle(j, _):
            cols = lanes(j * 256, 256)
            acc[0:size, cols] += jnp.dot(
                held[1, span(c), :], weight[block(far), cols], preferred_element_type=F32
            )
            return 0

        lax.fori_loop(0, tiles, middle, 0)
        fwd_copies[c].wait_recv()

        def last(j, _):
            cols = lanes(j * 256, 256)
            summed = acc[0:size, cols] + jnp.dot(
                held[2, span(c), :], weight[block(far_sib), cols], preferred_element_type=F32
            )
            proj[span(c), cols] = summed.astype(BF16)
            return 0

        lax.fori_loop(0, tiles, last, 0)

    @pl.when(me < 2)
    def _():
        chain_in[...] = jnp.zeros_like(chain_in)

    @pl.when(me == 0)
    def _():
        halo[...] = jnp.zeros_like(halo)

    pad_dec[...] = jnp.zeros_like(pad_dec)
    pad_dec[0, 0:heads, :] = decay_t[...]
    pad_dec[1, 0:heads, :] = decay_dot_t[...]
    t_index = lax.broadcasted_iota(jnp.int32, (SPAN, SPAN), 0)
    s_index = lax.broadcasted_iota(jnp.int32, (SPAN, SPAN), 1)
    upper = (t_index <= s_index).astype(F32)
    for b in range(blocks):
        at = slice(b * SPAN, (b + 1) * SPAN)
        for source, into, into_t in ((0, cum, cum_t), (1, cum_dot, cum_dot_t)):
            summed = jnp.dot(pad_dec[source, :, at], upper, precision=HIGHEST, preferred_element_type=F32)
            into_t[b] = summed
            into[at, :] = summed.T
    cum[length : length + 8, :] = jnp.zeros((8, 128), F32)
    cum[length : length + 1, 0:heads] = skip[...]

    def expand(p, _):
        cols = lanes(p * 128, 128)
        source = lax.broadcasted_iota(jnp.int32, (128, 128), 0)
        target = lax.broadcasted_iota(jnp.int32, (128, 128), 1)
        pick = (source == 2 * p + (target >= HEAD_DIM).astype(jnp.int32)).astype(F32)
        wide[:, cols] = jnp.dot(cum[...], pick, precision=HIGHEST, preferred_element_type=F32)
        wide_dot[:, cols] = jnp.dot(cum_dot[...], pick, precision=HIGHEST, preferred_element_type=F32)
        return 0

    lax.fori_loop(0, pairs, expand, 0)

    def convolve(b, cols, kernel, into, into_dot, to):
        start = b * SPAN
        convs = []
        for k in range(2):
            if b == 0:
                padded[k, 0:16, :] = halo[k, :, cols].astype(F32)
            else:
                padded[k, 0:16, :] = proj[k * length + start - 16 : k * length + start, cols].astype(F32)
            padded[k, 16 : 16 + SPAN, :] = proj[k * length + start : k * length + start + SPAN, cols].astype(F32)
            summed = kernel[0:1, :] * padded[k, 13 : 13 + SPAN, :]
            for tap in range(1, 4):
                summed = summed + kernel[tap : tap + 1, :] * padded[k, 13 + tap : 13 + tap + SPAN, :]
            convs.append(summed)
        gate = 1.0 / (1.0 + jnp.exp(-convs[0]))
        into[start : start + SPAN, to] = (convs[0] * gate).astype(BF16)
        into_dot[start : start + SPAN, to] = (
            convs[1] * (gate * (1.0 + convs[0] * (1.0 - gate)))
        ).astype(BF16)

    def convolve_all(b):
        for k in range(2):
            part = slice(k * state_len, (k + 1) * state_len)
            convolve(
                b, slice(width + k * state_len, width + (k + 1) * state_len), conv_bc[:, part], bc, bc_dot, part
            )

        def convolve_inner(p, _):
            cols = lanes(p * 128, 128)
            convolve(b, cols, conv_in[:, cols], x, x_dot, cols)
            return 0

        lax.fori_loop(0, pairs, convolve_inner, 0)

    def states_all(b):
        at = slice(b * SPAN, (b + 1) * SPAN)
        end = slice((b + 1) * SPAN - 1, (b + 1) * SPAN)
        writer_t = bc[at, 0:state_len].T
        writer_dot_t = bc_dot[at, 0:state_len].T

        def states(p, _):
            cols = lanes(p * 128, 128)
            last, last_dot = wide[end, cols], wide_dot[end, cols]
            remaining = jnp.exp(last - wide[at, cols])
            values = x[at, cols].astype(F32)
            scaled = (values * remaining).astype(BF16)
            scaled_dot = (
                (x_dot[at, cols].astype(F32) + values * (last_dot - wide_dot[at, cols])) * remaining
            ).astype(BF16)
            new = jnp.dot(writer_t, scaled, preferred_element_type=F32)
            new_dot = jnp.dot(writer_t, scaled_dot, preferred_element_type=F32) + jnp.dot(
                writer_dot_t, scaled, preferred_element_type=F32
            )
            state[b, :, cols] = new
            state_dot[b, :, cols] = new_dot
            if b == 0:
                final = slice(2 * SPAN - 1, 2 * SPAN)
                log, slope = wide[final, cols], wide_dot[final, cols]
                retain = jnp.exp(log)
                rows[p] = jnp.concatenate([last + log, last_dot + slope, jnp.zeros((6, 128), F32)], 0)
                total[p, 0] = (retain * new + state[1, :, cols]).astype(BF16)
                total[p, 1] = (retain * (new_dot + slope * new) + state_dot[1, :, cols]).astype(BF16)
            return 0

        lax.fori_loop(0, pairs, states, 0)

    def outer_t(left, right):
        return lax.dot_general(left, right, (((1,), (1,)), ((), ())), preferred_element_type=F32)

    def score_all(b):
        at = slice(b * SPAN, (b + 1) * SPAN)
        writer, reader = bc[at, 0:state_len], bc[at, state_len : 2 * state_len]
        writer_dot, reader_dot = bc_dot[at, 0:state_len], bc_dot[at, state_len : 2 * state_len]
        causal = t_index >= s_index
        score[b] = jnp.where(causal, outer_t(reader, writer), 0.0)
        score_dot[b] = jnp.where(causal, outer_t(reader_dot, writer) + outer_t(reader, writer_dot), 0.0)

    def mixing(b, p, _):
        cols = lanes(p * 128, 128)
        for t in range(SPAN // 128):
            size = (t + 1) * 128
            at = slice(b * SPAN + t * 128, b * SPAN + size)
            upto = slice(b * SPAN, b * SPAN + size)
            tile = slice(t * 128, size)
            values = x[upto, cols]
            both = jnp.concatenate([values, x_dot[upto, cols]], 1)
            column, column_dot = wide[at, cols], wide_dot[at, cols]
            found = []
            for k in range(2):
                first = k * HEAD_DIM
                row = cum_t[b, pl.ds(2 * p + k, 1), :][:, 0:size]
                row_dot = cum_dot_t[b, pl.ds(2 * p + k, 1), :][:, 0:size]
                weight = jnp.exp(jnp.minimum(column[:, first : first + 1] - row, 0.0))
                change = column_dot[:, first : first + 1] - row_dot
                scores = score[b, tile, 0:size]
                mix = (weight * scores).astype(BF16)
                mix_dot = (weight * (score_dot[b, tile, 0:size] + change * scores)).astype(BF16)
                found.append(
                    (
                        jnp.dot(mix, both, preferred_element_type=F32),
                        jnp.dot(mix_dot, values, preferred_element_type=F32),
                    )
                )
            (r0, q0), (r1, q1) = found
            within[at, cols] = jnp.where(lane < HEAD_DIM, r0[:, 0:128], r1[:, 0:128])
            within_dot[at, cols] = jnp.where(lane < HEAD_DIM, r0[:, 128:256] + q0, r1[:, 128:256] + q1)
        return 0

    halo_copies = [
        remote(
            proj.at[(k + 1) * length - 16 : (k + 1) * length, :],
            halo.at[k],
            halo_send.at[k],
            halo_recv.at[k],
            {"ctx": me + 1},
        )
        for k in range(2)
    ]
    for load in loads:
        load.wait()
    for c in (0, 1):
        near(c)
        forward(c)
        distant(c)

    @pl.when(me + 1 < count)
    def _():
        for copy in halo_copies:
            copy.start()

    convolve_all(1)
    states_all(1)
    score_all(1)
    lax.fori_loop(0, half, functools.partial(mixing, 1), 0)
    forward(2)
    lax.fori_loop(half, pairs, functools.partial(mixing, 1), 0)
    near(2)
    distant(2)
    near(3)
    forward(3)
    distant(3)

    out_half = p_near.shape[2]
    w_far = weight.at[0:width, 0:out_half]
    w_near = weight.at[width : 2 * width, 0:out_half]
    load_far = pltpu.make_async_copy(w_out.at[:, lanes((1 - chip) * out_half, out_half)], w_far, w_sem.at[3])
    load_near = pltpu.make_async_copy(w_out.at[:, lanes(chip * out_half, out_half)], w_near, w_sem.at[4])
    load_far.start()
    load_near.start()

    @pl.when(me > 0)
    def _():
        for copy in halo_copies:
            copy.wait_recv()

    convolve_all(0)
    states_all(0)

    mine = odd * half
    others = (1 - odd) * half
    pair_copies = [
        remote(total.at[pl.ds(others, half)], pair_total, pair_send.at[0], pair_recv.at[0], {"ctx": partner}),
        remote(rows.at[pl.ds(others, half)], pair_rows, pair_send.at[1], pair_recv.at[1], {"ctx": partner}),
    ]
    for copy in pair_copies:
        copy.start()
    score_all(0)
    lax.fori_loop(0, pairs, functools.partial(mixing, 0), 0)
    for copy in pair_copies:
        copy.wait_recv()

    chain_copies = [
        remote(chain_out.at[i], chain_in.at[i], chain_send.at[i], chain_recv.at[i], {"ctx": me + 2})
        for i in range(half)
    ]
    give_copies = [
        remote(give.at[i], entry.at[mine + i], give_send.at[i], give_recv.at[i], {"ctx": partner})
        for i in range(half)
    ]
    first_here = odd == 0
    for i in range(half):

        @pl.when(me >= 2)
        def _(i=i):
            chain_copies[i].wait_recv()

        arrived, arrived_dot = chain_in[i, 0].astype(F32), chain_in[i, 1].astype(F32)
        own, own_dot = total[mine + i, 0].astype(F32), total[mine + i, 1].astype(F32)
        their, their_dot = pair_total[i, 0].astype(F32), pair_total[i, 1].astype(F32)
        own_rows, their_rows = rows[mine + i], pair_rows[i]
        early_rows = jnp.where(first_here, own_rows, their_rows)
        late_rows = jnp.where(first_here, their_rows, own_rows)
        retain = jnp.exp(early_rows[0:1])
        middle = retain * arrived + jnp.where(first_here, own, their)
        middle_dot = retain * (arrived_dot + early_rows[1:2] * arrived) + jnp.where(
            first_here, own_dot, their_dot
        )
        retain = jnp.exp(late_rows[0:1])
        chain_out[i, 0] = (retain * middle + jnp.where(first_here, their, own)).astype(BF16)
        chain_out[i, 1] = (
            retain * (middle_dot + late_rows[1:2] * middle) + jnp.where(first_here, their_dot, own_dot)
        ).astype(BF16)

        @pl.when(me + 2 < count)
        def _(i=i):
            chain_copies[i].start()

        give[i, 0] = jnp.where(first_here, middle, arrived).astype(BF16)
        give[i, 1] = jnp.where(first_here, middle_dot, arrived_dot).astype(BF16)
        give_copies[i].start()
        entry[mine + i, 0] = jnp.where(first_here, arrived, middle).astype(BF16)
        entry[mine + i, 1] = jnp.where(first_here, arrived_dot, middle_dot).astype(BF16)

    def finish(p, _):
        cols = lanes(p * 128, 128)
        gain = wide[length : length + 1, cols]
        now, now_dot = entry[p, 0], entry[p, 1]
        for b in range(blocks):
            at = slice(b * SPAN, (b + 1) * SPAN)
            end = slice((b + 1) * SPAN - 1, (b + 1) * SPAN)
            reader = bc[at, state_len : 2 * state_len]
            reader_dot = bc_dot[at, state_len : 2 * state_len]
            read = jnp.dot(reader, jnp.concatenate([now, now_dot], 1), preferred_element_type=F32)
            moved = jnp.dot(reader_dot, now, preferred_element_type=F32)
            grown = jnp.exp(wide[at, cols])
            plain = read[:, 0:128]
            inner[at, cols] = (
                within[at, cols] + grown * plain + gain * x[at, cols].astype(F32)
            ).astype(BF16)
            inner[length + b * SPAN : length + (b + 1) * SPAN, cols] = (
                within_dot[at, cols]
                + grown * (read[:, 128:256] + moved + wide_dot[at, cols] * plain)
                + gain * x_dot[at, cols].astype(F32)
            ).astype(BF16)
            if b + 1 < blocks:
                retain = jnp.exp(wide[end, cols])
                old, old_dot = now.astype(F32), now_dot.astype(F32)
                now = (retain * old + state[b, :, cols]).astype(BF16)
                now_dot = (
                    retain * (old_dot + wide_dot[end, cols] * old) + state_dot[b, :, cols]
                ).astype(BF16)
        return 0

    lax.fori_loop(mine, mine + half, finish, 0)
    back_copies = [
        remote(give.at[i], entry.at[others + i], give_send.at[i], give_recv.at[i], {"ctx": partner})
        for i in range(half)
    ]
    for i in range(half):
        back_copies[i].wait_recv()
    lax.fori_loop(others, others + half, finish, 0)

    @pl.when(me + 1 < count)
    def _():
        for copy in halo_copies:
            copy.wait_send()

    keep = lanes(core * feat, feat)
    other_half = lanes((1 - core) * feat, feat)
    parts = 2 * length // SPAN

    def part(r):
        return slice(r * SPAN, (r + 1) * SPAN)

    a_copies = [
        remote(proj.at[part(r), other_half], r_far.at[r], a_send.at[r], a_recv.at[r], {"head": sib})
        for r in range(parts)
    ]
    x_copies = [
        remote(s_far.at[r], r_x.at[r], x_send.at[r], x_recv.at[r], {"head": far}) for r in range(parts)
    ]
    b_copies = [
        remote(p_near.at[r, :, other_half], r_near.at[r], b_send.at[r], b_recv.at[r], {"head": sib})
        for r in range(parts)
    ]

    def pass_on(r):
        a_copies[r].wait_recv()
        s_far[r] = (proj[part(r), keep].astype(F32) + r_far[r].astype(F32)).astype(BF16)
        x_copies[r].start()

    load_far.wait()
    load_near.wait()
    for r in range(parts):

        def far_tile(j, _, r=r):
            cols = lanes(j * 256, 256)
            proj[part(r), cols] = jnp.dot(
                inner[part(r), :], weight[0:width, cols], preferred_element_type=F32
            ).astype(BF16)
            return 0

        lax.fori_loop(0, out_half // 256, far_tile, 0)
        a_copies[r].start()
        if r > 0:
            pass_on(r - 1)
    for r in range(parts):

        def near_tile(j, _, r=r):
            cols = lanes(j * 256, 256)
            p_near[r, :, cols] = jnp.dot(
                inner[part(r), :], weight[width : 2 * width, cols], preferred_element_type=F32
            ).astype(BF16)
            return 0

        lax.fori_loop(0, out_half // 256, near_tile, 0)
        b_copies[r].start()
        if r == 0:
            pass_on(parts - 1)
    for r in range(parts):
        b_copies[r].wait_recv()
        x_copies[r].wait_recv()
        summed = p_near[r, :, keep].astype(F32) + r_near[r].astype(F32) + r_x[r].astype(F32)
        ref, at = (out, r) if r < parts // 2 else (out_dot, r - parts // 2)
        ref[part(at), :] = summed.astype(BF16)

    for copy in far_copies + sib_copies + fwd_copies + pair_copies + give_copies:
        copy.wait_send()
    for copy in a_copies + x_copies + b_copies:
        copy.wait_send()

    @pl.when(me + 2 < count)
    def _():
        for copy in chain_copies:
            copy.wait_send()


def fused_on_device(
    tokens, tangent_tokens, log_decay, tangent_decay, w_inner, w_bmat, w_cmat,
    conv_inner, conv_bc, skip_gain, w_out,
):
    length, feat = tokens.shape
    depth, width = w_inner.shape
    state_len = w_bmat.shape[1]
    full = width + 2 * state_len
    out_half = w_out.shape[1] // 2
    blocks = length // SPAN
    parts = 2 * blocks
    pairs = width // 128
    half = pairs // 2
    vmem = pl.BlockSpec(memory_space=pltpu.VMEM)
    anywhere = pl.BlockSpec(memory_space=pl.ANY)
    dma = pltpu.SemaphoreType.DMA
    piece = (2, state_len, 128)

    def bf16(*shape):
        return pltpu.VMEM(shape, BF16)

    def f32(*shape):
        return pltpu.VMEM(shape, F32)

    result = jax.ShapeDtypeStruct((length, feat), BF16)
    return pl.pallas_call(
        layer_kernel,
        out_shape=(result, result),
        in_specs=[vmem] * 4 + [anywhere] * 3 + [vmem] * 3 + [anywhere],
        out_specs=(vmem, vmem),
        scratch_shapes=[
            bf16(3, 2 * length, feat),
            f32(SPAN + 16, full),
            bf16(depth, full),
            bf16(2 * length, full),
            bf16(2 * length, width),
            bf16(2, 16, full),
            f32(2, 16 + SPAN, 128),
            f32(2, 128, length),
            f32(length + 8, 128),
            f32(length, 128),
            f32(blocks, 128, SPAN),
            f32(blocks, 128, SPAN),
            f32(length + 8, width),
            f32(length, width),
            bf16(length, width),
            bf16(length, width),
            bf16(length, 2 * state_len),
            bf16(length, 2 * state_len),
            f32(blocks, SPAN, SPAN),
            f32(blocks, SPAN, SPAN),
            f32(length, width),
            f32(length, width),
            f32(blocks, state_len, width),
            f32(blocks, state_len, width),
            bf16(pairs, *piece),
            f32(pairs, 8, 128),
            bf16(half, *piece),
            f32(half, 8, 128),
            bf16(half, *piece),
            bf16(half, *piece),
            bf16(half, *piece),
            bf16(pairs, *piece),
            bf16(parts, SPAN, out_half),
        ]
        + [bf16(parts, SPAN, feat)] * 4
        + [dma((5,))]
        + [dma((4,))] * 6
        + [dma((2,))] * 4
        + [dma((half,))] * 4
        + [dma((parts,))] * 6,
        compiler_params=pltpu.CompilerParams(
            collective_id=0, has_side_effects=True, vmem_limit_bytes=VMEM_LIMIT
        ),
        name="layer",
    )(
        tokens, tangent_tokens, log_decay.T, tangent_decay.T, w_inner, w_bmat, w_cmat,
        conv_inner, conv_bc, skip_gain.reshape(1, -1), w_out,
    )


def shifted(block, axis, distance):
    devices = range(lax.axis_size(axis))
    route = [(i - distance, i) for i in devices if i - distance in devices]
    return lax.ppermute(block, axis, route)


def carried_in(part, axis, combine, identity):
    place = lax.axis_index(axis)
    gathered = jax.tree.map(lambda a: lax.all_gather(a, axis), part)
    state = jax.tree.map(lambda a, e: jnp.zeros_like(a) + jnp.asarray(e, a.dtype), part, identity)

    def one(step, state):
        return combine(
            state, jax.tree.map(lambda a: lax.dynamic_index_in_dim(a, step, 0, False), gathered)
        )

    return lax.fori_loop(0, place, one, state)


def depthwise(padded, kernel):
    length = padded.shape[0] - kernel.shape[0] + 1
    summed = kernel[0] * padded[0:length]
    for offset in range(1, kernel.shape[0]):
        summed = summed + kernel[offset] * padded[offset : offset + length]
    return summed


def activate(values):
    return jax.nn.silu(values).astype(jnp.bfloat16)


def span_parts(inputs, writer, reader, decays):
    cumulative = jnp.cumsum(decays, axis=0)
    length = decays.shape[0]
    causal = lax.broadcasted_iota(jnp.int32, (length, length), 0) >= lax.broadcasted_iota(
        jnp.int32, (length, length), 1
    )
    differences = cumulative.T[:, :, None] - cumulative.T[:, None, :]
    weights = jnp.exp(jnp.where(causal[None], differences, -jnp.inf))
    scores = jnp.dot(reader, writer.T, preferred_element_type=jnp.float32)
    mixing = (weights * scores[None]).astype(jnp.bfloat16)
    within = jnp.einsum("hts,shp->thp", mixing, inputs, preferred_element_type=jnp.float32)
    remaining = jnp.exp(cumulative[-1][None, :] - cumulative)
    scaled = (inputs * remaining[:, :, None]).astype(jnp.bfloat16)
    block_state = jnp.einsum("shp,sn->hpn", scaled, writer, preferred_element_type=jnp.float32)
    return (cumulative, within, block_state)


def carried(reader, cumulative, initial):
    readout = jnp.einsum(
        "tn,hpn->thp", reader, initial.astype(jnp.bfloat16), preferred_element_type=jnp.float32
    )
    return jnp.exp(cumulative)[:, :, None] * readout


def combine(earlier, later):
    early_total, early_slope, early_state, early_tangent = earlier
    late_total, late_slope, late_state, late_tangent = later
    retain = jnp.exp(late_total)
    return (
        early_total + late_total,
        early_slope + late_slope,
        retain * early_state + late_state,
        retain * (early_tangent + late_slope * early_state) + late_tangent,
    )


def on_device(
    tokens,
    tangent_tokens,
    log_decay,
    tangent_decay,
    w_inner,
    w_bmat,
    w_cmat,
    conv_inner,
    conv_bc,
    skip_gain,
    w_out,
):
    length = tokens.shape[0]
    width = w_inner.shape[1]
    state_len = w_bmat.shape[1]
    heads_here = width // HEAD_DIM
    margin = conv_inner.shape[0] - 1
    blocks = length // SPAN
    stacked = jnp.concatenate([tokens, tangent_tokens], 0)
    shard_piece = lax.all_gather(stacked, "head", axis=1, tiled=True)
    sums = (
        jnp.dot(shard_piece, w_inner, preferred_element_type=jnp.float32),
        jnp.dot(shard_piece, w_bmat, preferred_element_type=jnp.float32),
        jnp.dot(shard_piece, w_cmat, preferred_element_type=jnp.float32),
    )
    projected = jnp.concatenate([summand.astype(jnp.bfloat16) for summand in sums], 1)
    edges = jnp.stack([projected[length - margin : length], projected[2 * length - margin :]])
    previous = shifted(edges, "ctx", 1)
    kernel = jnp.concatenate([conv_inner, conv_bc], 1)
    primal_conv = depthwise(jnp.concatenate([previous[0], projected[:length]], 0), kernel)
    tangent_conv = depthwise(jnp.concatenate([previous[1], projected[length:]], 0), kernel)
    mixed, mixed_dot = jax.jvp(activate, (primal_conv,), (tangent_conv,))

    def separate(values):
        inputs = values[:, :width].reshape(blocks, SPAN, heads_here, HEAD_DIM)
        writer = values[:, width : width + state_len].reshape(blocks, SPAN, state_len)
        reader = values[:, width + state_len :].reshape(blocks, SPAN, state_len)
        return (inputs, writer, reader)

    inputs, writer, reader = separate(mixed)
    inputs_dot, writer_dot, reader_dot = separate(mixed_dot)
    decays = log_decay.reshape(blocks, SPAN, heads_here)
    decays_dot = tangent_decay.reshape(blocks, SPAN, heads_here)
    (cumulative, within, block_state), (cumulative_dot, within_dot, block_dot) = jax.jvp(
        jax.vmap(span_parts),
        (inputs, writer, reader, decays),
        (inputs_dot, writer_dot, reader_dot, decays_dot),
    )

    def summarize(cumulative, block_state):
        summed = cumulative[0, -1]
        running = block_state[0]
        summed = summed + cumulative[1, -1]
        running = jnp.exp(cumulative[1, -1])[:, None, None] * running + block_state[1]
        return (summed[:, None, None], running)

    (decay_sum, own_state), (decay_sum_dot, own_dot) = jax.jvp(
        summarize, (cumulative, block_state), (cumulative_dot, block_dot)
    )
    message = (decay_sum, decay_sum_dot, own_state, own_dot)
    empty = tuple((jnp.zeros_like(member) for member in message))
    arriving = carried_in(message, "ctx", combine, empty)
    entry_state = arriving[2]
    entry_dot = arriving[3]

    def finish(initial, cumulative, within, block_state, inputs, reader):
        outputs = []
        for position in range(cumulative.shape[0]):
            combined = (
                within[position]
                + carried(reader[position], cumulative[position], initial)
                + skip_gain[None, :, None] * inputs[position]
            )
            outputs.append(combined.astype(jnp.bfloat16))
            if position + 1 < cumulative.shape[0]:
                initial = (
                    jnp.exp(cumulative[position, -1])[:, None, None] * initial
                    + block_state[position]
                )
        return jnp.stack(outputs)

    inner, inner_dot = jax.jvp(
        finish,
        (entry_state, cumulative, within, block_state, inputs, reader),
        (entry_dot, cumulative_dot, within_dot, block_dot, inputs_dot, reader_dot),
    )
    flattened = jnp.concatenate([inner.reshape(length, width), inner_dot.reshape(length, width)], 0)
    partial_term = jnp.dot(flattened, w_out, preferred_element_type=jnp.float32).astype(
        jnp.bfloat16
    )
    summed = (
        lax.psum_scatter(partial_term, "head", scatter_dimension=1, tiled=True)
        .astype(jnp.float32)
        .astype(jnp.bfloat16)
    )
    return (summed[:length], summed[length:])


def solution(mesh):
    in_specs = (
        P("ctx", "head"),
        P("ctx", "head"),
        P("ctx", "head"),
        P("ctx", "head"),
        P(None, "head"),
        P(),
        P(),
        P(None, "head"),
        P(),
        P("head"),
        P("head", None),
    )
    out_specs = (P("ctx", "head"), P("ctx", "head"))
    fits = mesh.shape["head"] == 4 and mesh.shape["ctx"] % 2 == 0
    return jax.shard_map(
        fused_on_device if fits else on_device, mesh=mesh, in_specs=in_specs, out_specs=out_specs, check_vma=False
    )
```

```python
import functools

import jax
import jax.numpy as jnp
from jax import lax
from jax.experimental import pallas as pl
from jax.experimental.pallas import tpu as pltpu
from jax.sharding import PartitionSpec as P

HEAD_DIM = 64
SPAN = 256
MESH = pl.DeviceIdType.MESH
HIGHEST = lax.Precision.HIGHEST
VMEM_LIMIT = 60 * 1024 * 1024
F32 = jnp.float32
BF16 = jnp.bfloat16


def remote(src, dst, send, recv, device):
    return pltpu.make_async_remote_copy(
        src_ref=src, dst_ref=dst, send_sem=send, recv_sem=recv, device_id=device, device_id_type=MESH
    )


def lanes(start, size):
    return pl.ds(pl.multiple_of(start, 128), size)


def layer_kernel(
    tok, tan, decay_t, decay_dot_t, w_in, w_b, w_c, conv_in, conv_bc, skip, w_out, out, out_dot,
    held, acc, weight, proj, inner,
    halo, padded, pad_dec, cum, cum_dot, cum_t, cum_dot_t, wide, wide_dot, x, x_dot, bc, bc_dot,
    score, score_dot, within, within_dot, state, state_dot,
    total, rows, pair_total, pair_rows, chain_in, chain_out, give, entry,
    p_near, r_far, s_far, r_x, r_near,
    w_sem, sib_send, sib_recv, far_send, far_recv, fwd_send, fwd_recv,
    halo_send, halo_recv, pair_send, pair_recv, chain_send, chain_recv, give_send, give_recv,
    a_send, a_recv, x_send, x_recv, b_send, b_recv,
):
    head = lax.axis_index("head")
    core = lax.rem(head, 2)
    chip = (head - core) // 2
    sib = head + 1 - 2 * core
    far = lax.rem(head + 2, 4)
    far_sib = lax.rem(sib + 2, 4)
    me = lax.axis_index("ctx")
    count = lax.axis_size("ctx")
    odd = lax.rem(me, 2)
    partner = me + 1 - 2 * odd
    length, feat = tok.shape
    width = x.shape[1]
    heads = decay_t.shape[0]
    pairs = width // 128
    half = pairs // 2
    blocks = length // SPAN
    state_len = bc.shape[1] // 2
    lane = lax.broadcasted_iota(jnp.int32, (1, 128), 1)

    loads = [
        pltpu.make_async_copy(w_in, weight.at[:, 0:width], w_sem.at[0]),
        pltpu.make_async_copy(w_b, weight.at[:, width : width + state_len], w_sem.at[1]),
        pltpu.make_async_copy(w_c, weight.at[:, width + state_len :], w_sem.at[2]),
    ]
    for load in loads:
        load.start()

    barrier = pltpu.get_barrier_semaphore()
    for other in (sib, far):
        pl.semaphore_signal(barrier, inc=1, device_id={"head": other}, device_id_type=MESH)
    for step in (-2, -1, 1, 2):
        other = me + step

        @pl.when(jnp.logical_and(other >= 0, other < count))
        def _(other=other):
            pl.semaphore_signal(barrier, inc=1, device_id={"ctx": other}, device_id_type=MESH)

    pl.semaphore_wait(barrier, 2 + jnp.minimum(me, 2) + jnp.minimum(count - 1 - me, 2))

    cut = length - SPAN - 16
    chunks = [(0, cut, length - cut), (1, cut, length - cut), (0, 0, cut), (1, 0, cut)]

    def own(c):
        k, start, size = chunks[c]
        return (tok, tan)[k].at[start : start + size]

    def span(c):
        k, start, size = chunks[c]
        return slice(k * length + start, k * length + start + size)

    order = range(len(chunks))
    far_copies = [
        remote(own(c), held.at[1, span(c)], far_send.at[c], far_recv.at[c], {"head": far}) for c in order
    ]
    sib_copies = [
        remote(own(c), held.at[0, span(c)], sib_send.at[c], sib_recv.at[c], {"head": sib}) for c in order
    ]
    fwd_copies = [
        remote(held.at[1, span(c)], held.at[2, span(c)], fwd_send.at[c], fwd_recv.at[c], {"head": sib})
        for c in order
    ]
    for c in order:
        far_copies[c].start()
        sib_copies[c].start()
    tiles = weight.shape[1] // 256

    def block(index):
        return pl.ds(pl.multiple_of(index * feat, 128), feat)

    def near(c):
        sib_copies[c].wait_recv()
        size = chunks[c][2]

        def one(j, _):
            cols = lanes(j * 256, 256)
            acc[0:size, cols] = jnp.dot(
                own(c)[...], weight[block(head), cols], preferred_element_type=F32
            ) + jnp.dot(held[0, span(c), :], weight[block(sib), cols], preferred_element_type=F32)
            return 0

        lax.fori_loop(0, tiles, one, 0)

    def forward(c):
        far_copies[c].wait_recv()
        fwd_copies[c].start()

    def distant(c):
        size = chunks[c][2]

        def middle(j, _):
            cols = lanes(j * 256, 256)
            acc[0:size, cols] += jnp.dot(
                held[1, span(c), :], weight[block(far), cols], preferred_element_type=F32
            )
            return 0

        lax.fori_loop(0, tiles, middle, 0)
        fwd_copies[c].wait_recv()

        def last(j, _):
            cols = lanes(j * 256, 256)
            summed = acc[0:size, cols] + jnp.dot(
                held[2, span(c), :], weight[block(far_sib), cols], preferred_element_type=F32
            )
            proj[span(c), cols] = summed.astype(BF16)
            return 0

        lax.fori_loop(0, tiles, last, 0)

    @pl.when(me < 2)
    def _():
        chain_in[...] = jnp.zeros_like(chain_in)

    @pl.when(me == 0)
    def _():
        halo[...] = jnp.zeros_like(halo)

    pad_dec[...] = jnp.zeros_like(pad_dec)
    pad_dec[0, 0:heads, :] = decay_t[...]
    pad_dec[1, 0:heads, :] = decay_dot_t[...]
    t_index = lax.broadcasted_iota(jnp.int32, (SPAN, SPAN), 0)
    s_index = lax.broadcasted_iota(jnp.int32, (SPAN, SPAN), 1)
    upper = (t_index <= s_index).astype(F32)
    for b in range(blocks):
        at = slice(b * SPAN, (b + 1) * SPAN)
        for source, into, into_t in ((0, cum, cum_t), (1, cum_dot, cum_dot_t)):
            summed = jnp.dot(pad_dec[source, :, at], upper, precision=HIGHEST, preferred_element_type=F32)
            into_t[b] = summed
            into[at, :] = summed.T
    cum[length : length + 8, :] = jnp.zeros((8, 128), F32)
    cum[length : length + 1, 0:heads] = skip[...]

    def expand(p, _):
        cols = lanes(p * 128, 128)
        source = lax.broadcasted_iota(jnp.int32, (128, 128), 0)
        target = lax.broadcasted_iota(jnp.int32, (128, 128), 1)
        pick = (source == 2 * p + (target >= HEAD_DIM).astype(jnp.int32)).astype(F32)
        wide[:, cols] = jnp.dot(cum[...], pick, precision=HIGHEST, preferred_element_type=F32)
        wide_dot[:, cols] = jnp.dot(cum_dot[...], pick, precision=HIGHEST, preferred_element_type=F32)
        return 0

    lax.fori_loop(0, pairs, expand, 0)

    def convolve(b, cols, kernel, into, into_dot, to):
        start = b * SPAN
        convs = []
        for k in range(2):
            if b == 0:
                padded[k, 0:16, :] = halo[k, :, cols].astype(F32)
            else:
                padded[k, 0:16, :] = proj[k * length + start - 16 : k * length + start, cols].astype(F32)
            padded[k, 16 : 16 + SPAN, :] = proj[k * length + start : k * length + start + SPAN, cols].astype(F32)
            summed = kernel[0:1, :] * padded[k, 13 : 13 + SPAN, :]
            for tap in range(1, 4):
                summed = summed + kernel[tap : tap + 1, :] * padded[k, 13 + tap : 13 + tap + SPAN, :]
            convs.append(summed)
        gate = 1.0 / (1.0 + jnp.exp(-convs[0]))
        into[start : start + SPAN, to] = (convs[0] * gate).astype(BF16)
        into_dot[start : start + SPAN, to] = (
            convs[1] * (gate * (1.0 + convs[0] * (1.0 - gate)))
        ).astype(BF16)

    def convolve_all(b):
        for k in range(2):
            part = slice(k * state_len, (k + 1) * state_len)
            convolve(
                b, slice(width + k * state_len, width + (k + 1) * state_len), conv_bc[:, part], bc, bc_dot, part
            )

        def convolve_inner(p, _):
            cols = lanes(p * 128, 128)
            convolve(b, cols, conv_in[:, cols], x, x_dot, cols)
            return 0

        lax.fori_loop(0, pairs, convolve_inner, 0)

    def states_all(b):
        at = slice(b * SPAN, (b + 1) * SPAN)
        end = slice((b + 1) * SPAN - 1, (b + 1) * SPAN)
        writer_t = bc[at, 0:state_len].T
        writer_dot_t = bc_dot[at, 0:state_len].T

        def states(p, _):
            cols = lanes(p * 128, 128)
            last, last_dot = wide[end, cols], wide_dot[end, cols]
            remaining = jnp.exp(last - wide[at, cols])
            values = x[at, cols].astype(F32)
            scaled = (values * remaining).astype(BF16)
            scaled_dot = (
                (x_dot[at, cols].astype(F32) + values * (last_dot - wide_dot[at, cols])) * remaining
            ).astype(BF16)
            new = jnp.dot(writer_t, scaled, preferred_element_type=F32)
            new_dot = jnp.dot(writer_t, scaled_dot, preferred_element_type=F32) + jnp.dot(
                writer_dot_t, scaled, preferred_element_type=F32
            )
            state[b, :, cols] = new
            state_dot[b, :, cols] = new_dot
            if b == 0:
                final = slice(2 * SPAN - 1, 2 * SPAN)
                log, slope = wide[final, cols], wide_dot[final, cols]
                retain = jnp.exp(log)
                rows[p] = jnp.concatenate([last + log, last_dot + slope, jnp.zeros((6, 128), F32)], 0)
                total[0, p] = (retain * new + state[1, :, cols]).astype(BF16)
                total[1, p] = (retain * (new_dot + slope * new) + state_dot[1, :, cols]).astype(BF16)
            return 0

        lax.fori_loop(0, pairs, states, 0)

    def outer_t(left, right):
        return lax.dot_general(left, right, (((1,), (1,)), ((), ())), preferred_element_type=F32)

    def score_all(b):
        at = slice(b * SPAN, (b + 1) * SPAN)
        writer, reader = bc[at, 0:state_len], bc[at, state_len : 2 * state_len]
        writer_dot, reader_dot = bc_dot[at, 0:state_len], bc_dot[at, state_len : 2 * state_len]
        causal = t_index >= s_index
        score[b] = jnp.where(causal, outer_t(reader, writer), 0.0)
        score_dot[b] = jnp.where(causal, outer_t(reader_dot, writer) + outer_t(reader, writer_dot), 0.0)

    def mixing(b, p, _):
        cols = lanes(p * 128, 128)
        for t in range(SPAN // 128):
            size = (t + 1) * 128
            at = slice(b * SPAN + t * 128, b * SPAN + size)
            upto = slice(b * SPAN, b * SPAN + size)
            tile = slice(t * 128, size)
            values = x[upto, cols]
            both = jnp.concatenate([values, x_dot[upto, cols]], 1)
            column, column_dot = wide[at, cols], wide_dot[at, cols]
            found = []
            for k in range(2):
                first = k * HEAD_DIM
                row = cum_t[b, pl.ds(2 * p + k, 1), :][:, 0:size]
                row_dot = cum_dot_t[b, pl.ds(2 * p + k, 1), :][:, 0:size]
                weight = jnp.exp(jnp.minimum(column[:, first : first + 1] - row, 0.0))
                change = column_dot[:, first : first + 1] - row_dot
                scores = score[b, tile, 0:size]
                mix = (weight * scores).astype(BF16)
                mix_dot = (weight * (score_dot[b, tile, 0:size] + change * scores)).astype(BF16)
                found.append(
                    (
                        jnp.dot(mix, both, preferred_element_type=F32),
                        jnp.dot(mix_dot, values, preferred_element_type=F32),
                    )
                )
            (r0, q0), (r1, q1) = found
            within[at, cols] = jnp.where(lane < HEAD_DIM, r0[:, 0:128], r1[:, 0:128])
            within_dot[at, cols] = jnp.where(lane < HEAD_DIM, r0[:, 128:256] + q0, r1[:, 128:256] + q1)
        return 0

    halo_copies = [
        remote(
            proj.at[(k + 1) * length - 16 : (k + 1) * length, :],
            halo.at[k],
            halo_send.at[k],
            halo_recv.at[k],
            {"ctx": me + 1},
        )
        for k in range(2)
    ]
    for load in loads:
        load.wait()
    for c in (0, 1):
        near(c)
        forward(c)
        distant(c)

    @pl.when(me + 1 < count)
    def _():
        for copy in halo_copies:
            copy.start()

    convolve_all(1)
    states_all(1)
    score_all(1)
    lax.fori_loop(0, half, functools.partial(mixing, 1), 0)
    forward(2)
    lax.fori_loop(half, pairs, functools.partial(mixing, 1), 0)
    near(2)
    distant(2)
    near(3)
    forward(3)
    distant(3)

    out_half = p_near.shape[2]
    w_far = weight.at[0:width, 0:out_half]
    w_near = weight.at[width : 2 * width, 0:out_half]
    load_far = pltpu.make_async_copy(w_out.at[:, lanes((1 - chip) * out_half, out_half)], w_far, w_sem.at[3])
    load_near = pltpu.make_async_copy(w_out.at[:, lanes(chip * out_half, out_half)], w_near, w_sem.at[4])
    load_far.start()
    load_near.start()

    @pl.when(me > 0)
    def _():
        for copy in halo_copies:
            copy.wait_recv()

    convolve_all(0)
    states_all(0)

    mine = odd * half
    others = (1 - odd) * half
    def pair_copy(source, into, k):
        return remote(source, into, pair_send.at[k], pair_recv.at[k], {"ctx": partner})

    pair_copies = [
        pair_copy(total.at[0, pl.ds(others, half)], pair_total.at[0], 0),
        pair_copy(rows.at[pl.ds(others, half)], pair_rows, 1),
        pair_copy(total.at[1, pl.ds(others, half)], pair_total.at[1], 2),
    ]
    for copy in pair_copies:
        copy.start()
    score_all(0)
    lax.fori_loop(0, pairs, functools.partial(mixing, 0), 0)
    chain_copies = [
        [
            remote(chain_out.at[k, i], chain_in.at[k, i], chain_send.at[k, i], chain_recv.at[k, i], {"ctx": me + 2})
            for i in range(half)
        ]
        for k in range(2)
    ]
    give_copies = [
        [
            remote(give.at[k, i], entry.at[k, mine + i], give_send.at[k, i], give_recv.at[k, i], {"ctx": partner})
            for i in range(half)
        ]
        for k in range(2)
    ]
    back_copies = [
        [
            remote(give.at[k, i], entry.at[k, others + i], give_send.at[k, i], give_recv.at[k, i], {"ctx": partner})
            for i in range(half)
        ]
        for k in range(2)
    ]
    first_here = odd == 0

    def ordered(own_part, their_part):
        return (
            jnp.where(first_here, own_part, their_part),
            jnp.where(first_here, their_part, own_part),
        )

    def link(k, i):
        @pl.when(me >= 2)
        def _():
            chain_copies[k][i].wait_recv()

        early_rows, late_rows = ordered(rows[mine + i], pair_rows[i])
        keep_early, keep_late = jnp.exp(early_rows[0:1]), jnp.exp(late_rows[0:1])
        early, late = ordered(total[0, mine + i].astype(F32), pair_total[0, i].astype(F32))
        arrived = chain_in[0, i].astype(F32)
        middle = keep_early * arrived + early
        leaving = keep_late * middle + late
        if k == 1:
            early, late = ordered(total[1, mine + i].astype(F32), pair_total[1, i].astype(F32))
            slope_early, slope_late = early_rows[1:2], late_rows[1:2]
            before = arrived
            arrived = chain_in[1, i].astype(F32)
            leaving = keep_early * (arrived + slope_early * before) + early
            leaving, middle = keep_late * (leaving + slope_late * middle) + late, leaving
        chain_out[k, i] = leaving.astype(BF16)

        @pl.when(me + 2 < count)
        def _():
            chain_copies[k][i].start()

        give[k, i] = jnp.where(first_here, middle, arrived).astype(BF16)
        give_copies[k][i].start()
        entry[k, mine + i] = jnp.where(first_here, arrived, middle).astype(BF16)

    def finish(p, _):
        cols = lanes(p * 128, 128)
        gain = wide[length : length + 1, cols]
        now = entry[0, p]
        for b in range(blocks):
            at = slice(b * SPAN, (b + 1) * SPAN)
            end = slice((b + 1) * SPAN - 1, (b + 1) * SPAN)
            read = jnp.dot(bc[at, state_len : 2 * state_len], now, preferred_element_type=F32)
            inner[at, cols] = (
                within[at, cols] + jnp.exp(wide[at, cols]) * read + gain * x[at, cols].astype(F32)
            ).astype(BF16)
            if b + 1 < blocks:
                now = (jnp.exp(wide[end, cols]) * now.astype(F32) + state[b, :, cols]).astype(BF16)
        return 0

    def finish_dot(p, _):
        cols = lanes(p * 128, 128)
        gain = wide[length : length + 1, cols]
        now, now_dot = entry[0, p], entry[1, p]
        for b in range(blocks):
            at = slice(b * SPAN, (b + 1) * SPAN)
            end = slice((b + 1) * SPAN - 1, (b + 1) * SPAN)
            reader = bc[at, state_len : 2 * state_len]
            reader_dot = bc_dot[at, state_len : 2 * state_len]
            read = jnp.dot(reader, jnp.concatenate([now, now_dot], 1), preferred_element_type=F32)
            moved = jnp.dot(reader_dot, now, preferred_element_type=F32)
            inner[length + b * SPAN : length + (b + 1) * SPAN, cols] = (
                within_dot[at, cols]
                + jnp.exp(wide[at, cols])
                * (read[:, 128:256] + moved + wide_dot[at, cols] * read[:, 0:128])
                + gain * x_dot[at, cols].astype(F32)
            ).astype(BF16)
            if b + 1 < blocks:
                retain = jnp.exp(wide[end, cols])
                old, old_dot = now.astype(F32), now_dot.astype(F32)
                now = (retain * old + state[b, :, cols]).astype(BF16)
                now_dot = (
                    retain * (old_dot + wide_dot[end, cols] * old) + state_dot[b, :, cols]
                ).astype(BF16)
        return 0

    keep = lanes(core * feat, feat)
    other_half = lanes((1 - core) * feat, feat)
    parts = 2 * length // SPAN

    def part(r):
        return slice(r * SPAN, (r + 1) * SPAN)

    a_copies = [
        remote(proj.at[part(r), other_half], r_far.at[r], a_send.at[r], a_recv.at[r], {"head": sib})
        for r in range(parts)
    ]
    x_copies = [
        remote(s_far.at[r], r_x.at[r], x_send.at[r], x_recv.at[r], {"head": far}) for r in range(parts)
    ]
    b_copies = [
        remote(p_near.at[r, :, other_half], r_near.at[r], b_send.at[r], b_recv.at[r], {"head": sib})
        for r in range(parts)
    ]

    def pass_on(r):
        a_copies[r].wait_recv()
        s_far[r] = (proj[part(r), keep].astype(F32) + r_far[r].astype(F32)).astype(BF16)
        x_copies[r].start()

    def far_terms(r):
        def one(j, _):
            cols = lanes(j * 256, 256)
            proj[part(r), cols] = jnp.dot(
                inner[part(r), :], weight[0:width, cols], preferred_element_type=F32
            ).astype(BF16)
            return 0

        lax.fori_loop(0, out_half // 256, one, 0)
        a_copies[r].start()

    def near_terms(r):
        def one(j, _):
            cols = lanes(j * 256, 256)
            p_near[r, :, cols] = jnp.dot(
                inner[part(r), :], weight[width : 2 * width, cols], preferred_element_type=F32
            ).astype(BF16)
            return 0

        lax.fori_loop(0, out_half // 256, one, 0)
        b_copies[r].start()

    pair_copies[0].wait_recv()
    pair_copies[1].wait_recv()
    for i in range(half):
        link(0, i)
    lax.fori_loop(mine, mine + half, finish, 0)
    load_far.wait()
    load_near.wait()

    @pl.when(me + 1 < count)
    def _():
        for copy in halo_copies:
            copy.wait_send()

    for i in range(half):
        back_copies[0][i].wait_recv()
    lax.fori_loop(others, others + half, finish, 0)
    far_terms(0)
    far_terms(1)
    pass_on(0)
    pair_copies[2].wait_recv()
    near_terms(0)
    pass_on(1)
    for i in range(half):
        link(1, i)
    lax.fori_loop(mine, mine + half, finish_dot, 0)
    for i in range(half):
        back_copies[1][i].wait_recv()
    lax.fori_loop(others, others + half, finish_dot, 0)
    far_terms(2)
    far_terms(3)
    pass_on(2)
    near_terms(1)
    pass_on(3)
    near_terms(2)
    near_terms(3)
    for r in range(parts):
        b_copies[r].wait_recv()
        x_copies[r].wait_recv()
        summed = p_near[r, :, keep].astype(F32) + r_near[r].astype(F32) + r_x[r].astype(F32)
        ref, at = (out, r) if r < parts // 2 else (out_dot, r - parts // 2)
        ref[part(at), :] = summed.astype(BF16)

    for copy in far_copies + sib_copies + fwd_copies + pair_copies + give_copies[0] + give_copies[1]:
        copy.wait_send()
    for copy in a_copies + x_copies + b_copies:
        copy.wait_send()

    @pl.when(me + 2 < count)
    def _():
        for copy in chain_copies[0] + chain_copies[1]:
            copy.wait_send()


def place_kernel(values, values_dot, out, out_dot):
    out[...] = values[...]
    out_dot[...] = values_dot[...]


def fused_on_device(
    tokens, tangent_tokens, log_decay, tangent_decay, w_inner, w_bmat, w_cmat,
    conv_inner, conv_bc, skip_gain, w_out,
):
    length, feat = tokens.shape
    depth, width = w_inner.shape
    state_len = w_bmat.shape[1]
    full = width + 2 * state_len
    out_half = w_out.shape[1] // 2
    blocks = length // SPAN
    parts = 2 * blocks
    pairs = width // 128
    half = pairs // 2
    vmem = pl.BlockSpec(memory_space=pltpu.VMEM)
    anywhere = pl.BlockSpec(memory_space=pl.ANY)
    dma = pltpu.SemaphoreType.DMA
    piece = (state_len, 128)

    def bf16(*shape):
        return pltpu.VMEM(shape, BF16)

    def f32(*shape):
        return pltpu.VMEM(shape, F32)

    result = jax.ShapeDtypeStruct((length, feat), BF16)
    outputs = pl.pallas_call(
        layer_kernel,
        out_shape=(result, result),
        in_specs=[vmem] * 4 + [anywhere] * 3 + [vmem] * 3 + [anywhere],
        out_specs=(vmem, vmem),
        scratch_shapes=[
            bf16(3, 2 * length, feat),
            f32(SPAN + 16, full),
            bf16(depth, full),
            bf16(2 * length, full),
            bf16(2 * length, width),
            bf16(2, 16, full),
            f32(2, 16 + SPAN, 128),
            f32(2, 128, length),
            f32(length + 8, 128),
            f32(length, 128),
            f32(blocks, 128, SPAN),
            f32(blocks, 128, SPAN),
            f32(length + 8, width),
            f32(length, width),
            bf16(length, width),
            bf16(length, width),
            bf16(length, 2 * state_len),
            bf16(length, 2 * state_len),
            f32(blocks, SPAN, SPAN),
            f32(blocks, SPAN, SPAN),
            f32(length, width),
            f32(length, width),
            f32(blocks, state_len, width),
            f32(blocks, state_len, width),
            bf16(2, pairs, *piece),
            f32(pairs, 8, 128),
            bf16(2, half, *piece),
            f32(half, 8, 128),
            bf16(2, half, *piece),
            bf16(2, half, *piece),
            bf16(2, half, *piece),
            bf16(2, pairs, *piece),
            bf16(parts, SPAN, out_half),
        ]
        + [bf16(parts, SPAN, feat)] * 4
        + [dma((5,))]
        + [dma((4,))] * 6
        + [dma((2,))] * 2
        + [dma((3,))] * 2
        + [dma((2, half))] * 4
        + [dma((parts,))] * 6,
        compiler_params=pltpu.CompilerParams(
            collective_id=0, has_side_effects=True, vmem_limit_bytes=VMEM_LIMIT
        ),
        name="layer",
    )(
        tokens, tangent_tokens, log_decay.T, tangent_decay.T, w_inner, w_bmat, w_cmat,
        conv_inner, conv_bc, skip_gain.reshape(1, -1), w_out,
    )
    return pl.pallas_call(
        place_kernel,
        out_shape=(result, result),
        in_specs=[vmem, vmem],
        out_specs=(vmem, vmem),
        compiler_params=pltpu.CompilerParams(vmem_limit_bytes=16 * 1024 * 1024),
        name="place",
    )(*outputs)


def shifted(block, axis, distance):
    devices = range(lax.axis_size(axis))
    route = [(i - distance, i) for i in devices if i - distance in devices]
    return lax.ppermute(block, axis, route)


def carried_in(part, axis, combine, identity):
    place = lax.axis_index(axis)
    gathered = jax.tree.map(lambda a: lax.all_gather(a, axis), part)
    state = jax.tree.map(lambda a, e: jnp.zeros_like(a) + jnp.asarray(e, a.dtype), part, identity)

    def one(step, state):
        return combine(
            state, jax.tree.map(lambda a: lax.dynamic_index_in_dim(a, step, 0, False), gathered)
        )

    return lax.fori_loop(0, place, one, state)


def depthwise(padded, kernel):
    length = padded.shape[0] - kernel.shape[0] + 1
    summed = kernel[0] * padded[0:length]
    for offset in range(1, kernel.shape[0]):
        summed = summed + kernel[offset] * padded[offset : offset + length]
    return summed


def activate(values):
    return jax.nn.silu(values).astype(jnp.bfloat16)


def span_parts(inputs, writer, reader, decays):
    cumulative = jnp.cumsum(decays, axis=0)
    length = decays.shape[0]
    causal = lax.broadcasted_iota(jnp.int32, (length, length), 0) >= lax.broadcasted_iota(
        jnp.int32, (length, length), 1
    )
    differences = cumulative.T[:, :, None] - cumulative.T[:, None, :]
    weights = jnp.exp(jnp.where(causal[None], differences, -jnp.inf))
    scores = jnp.dot(reader, writer.T, preferred_element_type=jnp.float32)
    mixing = (weights * scores[None]).astype(jnp.bfloat16)
    within = jnp.einsum("hts,shp->thp", mixing, inputs, preferred_element_type=jnp.float32)
    remaining = jnp.exp(cumulative[-1][None, :] - cumulative)
    scaled = (inputs * remaining[:, :, None]).astype(jnp.bfloat16)
    block_state = jnp.einsum("shp,sn->hpn", scaled, writer, preferred_element_type=jnp.float32)
    return (cumulative, within, block_state)


def carried(reader, cumulative, initial):
    readout = jnp.einsum(
        "tn,hpn->thp", reader, initial.astype(jnp.bfloat16), preferred_element_type=jnp.float32
    )
    return jnp.exp(cumulative)[:, :, None] * readout


def combine(earlier, later):
    early_total, early_slope, early_state, early_tangent = earlier
    late_total, late_slope, late_state, late_tangent = later
    retain = jnp.exp(late_total)
    return (
        early_total + late_total,
        early_slope + late_slope,
        retain * early_state + late_state,
        retain * (early_tangent + late_slope * early_state) + late_tangent,
    )


def on_device(
    tokens,
    tangent_tokens,
    log_decay,
    tangent_decay,
    w_inner,
    w_bmat,
    w_cmat,
    conv_inner,
    conv_bc,
    skip_gain,
    w_out,
):
    length = tokens.shape[0]
    width = w_inner.shape[1]
    state_len = w_bmat.shape[1]
    heads_here = width // HEAD_DIM
    margin = conv_inner.shape[0] - 1
    blocks = length // SPAN
    stacked = jnp.concatenate([tokens, tangent_tokens], 0)
    shard_piece = lax.all_gather(stacked, "head", axis=1, tiled=True)
    sums = (
        jnp.dot(shard_piece, w_inner, preferred_element_type=jnp.float32),
        jnp.dot(shard_piece, w_bmat, preferred_element_type=jnp.float32),
        jnp.dot(shard_piece, w_cmat, preferred_element_type=jnp.float32),
    )
    projected = jnp.concatenate([summand.astype(jnp.bfloat16) for summand in sums], 1)
    edges = jnp.stack([projected[length - margin : length], projected[2 * length - margin :]])
    previous = shifted(edges, "ctx", 1)
    kernel = jnp.concatenate([conv_inner, conv_bc], 1)
    primal_conv = depthwise(jnp.concatenate([previous[0], projected[:length]], 0), kernel)
    tangent_conv = depthwise(jnp.concatenate([previous[1], projected[length:]], 0), kernel)
    mixed, mixed_dot = jax.jvp(activate, (primal_conv,), (tangent_conv,))

    def separate(values):
        inputs = values[:, :width].reshape(blocks, SPAN, heads_here, HEAD_DIM)
        writer = values[:, width : width + state_len].reshape(blocks, SPAN, state_len)
        reader = values[:, width + state_len :].reshape(blocks, SPAN, state_len)
        return (inputs, writer, reader)

    inputs, writer, reader = separate(mixed)
    inputs_dot, writer_dot, reader_dot = separate(mixed_dot)
    decays = log_decay.reshape(blocks, SPAN, heads_here)
    decays_dot = tangent_decay.reshape(blocks, SPAN, heads_here)
    (cumulative, within, block_state), (cumulative_dot, within_dot, block_dot) = jax.jvp(
        jax.vmap(span_parts),
        (inputs, writer, reader, decays),
        (inputs_dot, writer_dot, reader_dot, decays_dot),
    )

    def summarize(cumulative, block_state):
        summed = cumulative[0, -1]
        running = block_state[0]
        summed = summed + cumulative[1, -1]
        running = jnp.exp(cumulative[1, -1])[:, None, None] * running + block_state[1]
        return (summed[:, None, None], running)

    (decay_sum, own_state), (decay_sum_dot, own_dot) = jax.jvp(
        summarize, (cumulative, block_state), (cumulative_dot, block_dot)
    )
    message = (decay_sum, decay_sum_dot, own_state, own_dot)
    empty = tuple((jnp.zeros_like(member) for member in message))
    arriving = carried_in(message, "ctx", combine, empty)
    entry_state = arriving[2]
    entry_dot = arriving[3]

    def finish(initial, cumulative, within, block_state, inputs, reader):
        outputs = []
        for position in range(cumulative.shape[0]):
            combined = (
                within[position]
                + carried(reader[position], cumulative[position], initial)
                + skip_gain[None, :, None] * inputs[position]
            )
            outputs.append(combined.astype(jnp.bfloat16))
            if position + 1 < cumulative.shape[0]:
                initial = (
                    jnp.exp(cumulative[position, -1])[:, None, None] * initial
                    + block_state[position]
                )
        return jnp.stack(outputs)

    inner, inner_dot = jax.jvp(
        finish,
        (entry_state, cumulative, within, block_state, inputs, reader),
        (entry_dot, cumulative_dot, within_dot, block_dot, inputs_dot, reader_dot),
    )
    flattened = jnp.concatenate([inner.reshape(length, width), inner_dot.reshape(length, width)], 0)
    partial_term = jnp.dot(flattened, w_out, preferred_element_type=jnp.float32).astype(
        jnp.bfloat16
    )
    summed = (
        lax.psum_scatter(partial_term, "head", scatter_dimension=1, tiled=True)
        .astype(jnp.float32)
        .astype(jnp.bfloat16)
    )
    return (summed[:length], summed[length:])


def solution(mesh):
    in_specs = (
        P("ctx", "head"),
        P("ctx", "head"),
        P("ctx", "head"),
        P("ctx", "head"),
        P(None, "head"),
        P(),
        P(),
        P(None, "head"),
        P(),
        P("head"),
        P("head", None),
    )
    out_specs = (P("ctx", "head"), P("ctx", "head"))
    fits = mesh.shape["head"] == 4 and mesh.shape["ctx"] % 2 == 0
    return jax.shard_map(
        fused_on_device if fits else on_device, mesh=mesh, in_specs=in_specs, out_specs=out_specs, check_vma=False
    )
```

```python
import functools

import jax
import jax.numpy as jnp
from jax import lax
from jax.experimental import pallas as pl
from jax.experimental.pallas import tpu as pltpu
from jax.sharding import PartitionSpec as P

HEAD_DIM = 64
SPAN = 256
MESH = pl.DeviceIdType.MESH
HIGHEST = lax.Precision.HIGHEST
VMEM_LIMIT = 60 * 1024 * 1024
F32 = jnp.float32
BF16 = jnp.bfloat16


def remote(src, dst, send, recv, device):
    return pltpu.make_async_remote_copy(
        src_ref=src, dst_ref=dst, send_sem=send, recv_sem=recv, device_id=device, device_id_type=MESH
    )


def lanes(start, size):
    return pl.ds(pl.multiple_of(start, 128), size)


def layer_kernel(
    tok, tan, decay_t, decay_dot_t, w_in, w_b, w_c, conv_in, conv_bc, skip, w_out, out, out_dot,
    held, acc, weight, proj, inner,
    halo, padded, pad_dec, cum, cum_dot, cum_t, cum_dot_t, wide, wide_dot, x, x_dot, bc, bc_dot,
    score, score_dot, within, within_dot, state, state_dot,
    total, rows, pair_total, pair_rows, chain_in, chain_out, give, entry,
    p_near, r_far, s_far, r_x, r_near, staged, own_tok, own_tan,
    store_sem, w_sem, sib_send, sib_recv, far_send, far_recv, fwd_send, fwd_recv,
    halo_send, halo_recv, pair_send, pair_recv, chain_send, chain_recv, give_send, give_recv,
    a_send, a_recv, x_send, x_recv, b_send, b_recv,
):
    head = lax.axis_index("head")
    core = lax.rem(head, 2)
    chip = (head - core) // 2
    sib = head + 1 - 2 * core
    far = lax.rem(head + 2, 4)
    far_sib = lax.rem(sib + 2, 4)
    me = lax.axis_index("ctx")
    count = lax.axis_size("ctx")
    odd = lax.rem(me, 2)
    partner = me + 1 - 2 * odd
    length, feat = tok.shape
    width = x.shape[1]
    heads = decay_t.shape[0]
    pairs = width // 128
    half = pairs // 2
    blocks = length // SPAN
    state_len = bc.shape[1] // 2
    lane = lax.broadcasted_iota(jnp.int32, (1, 128), 1)

    loads = [
        pltpu.make_async_copy(tok, own_tok, w_sem.at[5]),
        pltpu.make_async_copy(tan, own_tan, w_sem.at[6]),
        pltpu.make_async_copy(w_in, weight.at[:, 0:width], w_sem.at[0]),
        pltpu.make_async_copy(w_b, weight.at[:, width : width + state_len], w_sem.at[1]),
        pltpu.make_async_copy(w_c, weight.at[:, width + state_len :], w_sem.at[2]),
    ]
    for load in loads:
        load.start()

    barrier = pltpu.get_barrier_semaphore()
    for other in (sib, far):
        pl.semaphore_signal(barrier, inc=1, device_id={"head": other}, device_id_type=MESH)
    for step in (-2, -1, 1, 2):
        other = me + step

        @pl.when(jnp.logical_and(other >= 0, other < count))
        def _(other=other):
            pl.semaphore_signal(barrier, inc=1, device_id={"ctx": other}, device_id_type=MESH)

    pl.semaphore_wait(barrier, 2 + jnp.minimum(me, 2) + jnp.minimum(count - 1 - me, 2))

    cut = length - SPAN - 16
    chunks = [(0, cut, length - cut), (1, cut, length - cut), (0, 0, cut), (1, 0, cut)]

    def own(c):
        k, start, size = chunks[c]
        return (tok, tan)[k].at[start : start + size]

    def own_values(c):
        k, start, size = chunks[c]
        return (own_tok, own_tan)[k][start : start + size, :]

    def span(c):
        k, start, size = chunks[c]
        return slice(k * length + start, k * length + start + size)

    order = range(len(chunks))
    far_copies = [
        remote(own(c), held.at[1, span(c)], far_send.at[c], far_recv.at[c], {"head": far}) for c in order
    ]
    sib_copies = [
        remote(own(c), held.at[0, span(c)], sib_send.at[c], sib_recv.at[c], {"head": sib}) for c in order
    ]
    fwd_copies = [
        remote(held.at[1, span(c)], held.at[2, span(c)], fwd_send.at[c], fwd_recv.at[c], {"head": sib})
        for c in order
    ]
    for c in order:
        far_copies[c].start()
        sib_copies[c].start()
    tiles = weight.shape[1] // 256

    def block(index):
        return pl.ds(pl.multiple_of(index * feat, 128), feat)

    def near(c):
        sib_copies[c].wait_recv()
        size = chunks[c][2]

        def one(j, _):
            cols = lanes(j * 256, 256)
            acc[0:size, cols] = jnp.dot(
                own_values(c), weight[block(head), cols], preferred_element_type=F32
            ) + jnp.dot(held[0, span(c), :], weight[block(sib), cols], preferred_element_type=F32)
            return 0

        lax.fori_loop(0, tiles, one, 0)

    def forward(c):
        far_copies[c].wait_recv()
        fwd_copies[c].start()

    def distant(c):
        size = chunks[c][2]

        def middle(j, _):
            cols = lanes(j * 256, 256)
            acc[0:size, cols] += jnp.dot(
                held[1, span(c), :], weight[block(far), cols], preferred_element_type=F32
            )
            return 0

        lax.fori_loop(0, tiles, middle, 0)
        fwd_copies[c].wait_recv()

        def last(j, _):
            cols = lanes(j * 256, 256)
            summed = acc[0:size, cols] + jnp.dot(
                held[2, span(c), :], weight[block(far_sib), cols], preferred_element_type=F32
            )
            proj[span(c), cols] = summed.astype(BF16)
            return 0

        lax.fori_loop(0, tiles, last, 0)

    @pl.when(me < 2)
    def _():
        chain_in[...] = jnp.zeros_like(chain_in)

    @pl.when(me == 0)
    def _():
        halo[...] = jnp.zeros_like(halo)

    pad_dec[...] = jnp.zeros_like(pad_dec)
    pad_dec[0, 0:heads, :] = decay_t[...]
    pad_dec[1, 0:heads, :] = decay_dot_t[...]
    t_index = lax.broadcasted_iota(jnp.int32, (SPAN, SPAN), 0)
    s_index = lax.broadcasted_iota(jnp.int32, (SPAN, SPAN), 1)
    upper = (t_index <= s_index).astype(F32)
    for b in range(blocks):
        at = slice(b * SPAN, (b + 1) * SPAN)
        for source, into, into_t in ((0, cum, cum_t), (1, cum_dot, cum_dot_t)):
            summed = jnp.dot(pad_dec[source, :, at], upper, precision=HIGHEST, preferred_element_type=F32)
            into_t[b] = summed
            into[at, :] = summed.T
    cum[length : length + 8, :] = jnp.zeros((8, 128), F32)
    cum[length : length + 1, 0:heads] = skip[...]

    def expand(p, _):
        cols = lanes(p * 128, 128)
        source = lax.broadcasted_iota(jnp.int32, (128, 128), 0)
        target = lax.broadcasted_iota(jnp.int32, (128, 128), 1)
        pick = (source == 2 * p + (target >= HEAD_DIM).astype(jnp.int32)).astype(F32)
        wide[:, cols] = jnp.dot(cum[...], pick, precision=HIGHEST, preferred_element_type=F32)
        wide_dot[:, cols] = jnp.dot(cum_dot[...], pick, precision=HIGHEST, preferred_element_type=F32)
        return 0

    lax.fori_loop(0, pairs, expand, 0)

    def convolve(b, wanted, cols, kernel, into, into_dot, to):
        start = b * SPAN
        convs = []
        for k in range(1 + max(wanted)):
            if b == 0:
                padded[k, 0:16, :] = halo[k, :, cols].astype(F32)
            else:
                padded[k, 0:16, :] = proj[k * length + start - 16 : k * length + start, cols].astype(F32)
            padded[k, 16 : 16 + SPAN, :] = proj[k * length + start : k * length + start + SPAN, cols].astype(F32)
            summed = kernel[0:1, :] * padded[k, 13 : 13 + SPAN, :]
            for tap in range(1, 4):
                summed = summed + kernel[tap : tap + 1, :] * padded[k, 13 + tap : 13 + tap + SPAN, :]
            convs.append(summed)
        gate = 1.0 / (1.0 + jnp.exp(-convs[0]))
        if 0 in wanted:
            into[start : start + SPAN, to] = (convs[0] * gate).astype(BF16)
        if 1 in wanted:
            into_dot[start : start + SPAN, to] = (
                convs[1] * (gate * (1.0 + convs[0] * (1.0 - gate)))
            ).astype(BF16)

    def convolve_all(b, wanted):
        for k in range(2):
            part = slice(k * state_len, (k + 1) * state_len)
            convolve(
                b, wanted, slice(width + k * state_len, width + (k + 1) * state_len), conv_bc[:, part], bc, bc_dot, part
            )

        def convolve_inner(p, _):
            cols = lanes(p * 128, 128)
            convolve(b, wanted, cols, conv_in[:, cols], x, x_dot, cols)
            return 0

        lax.fori_loop(0, pairs, convolve_inner, 0)

    def states_all(b, wanted):
        at = slice(b * SPAN, (b + 1) * SPAN)
        end = slice((b + 1) * SPAN - 1, (b + 1) * SPAN)
        final = slice(2 * SPAN - 1, 2 * SPAN)
        writer_t = bc[at, 0:state_len].T
        writer_dot_t = bc_dot[at, 0:state_len].T if 1 in wanted else None

        def states(p, _):
            cols = lanes(p * 128, 128)
            last, last_dot = wide[end, cols], wide_dot[end, cols]
            log, slope = wide[final, cols], wide_dot[final, cols]
            retain = jnp.exp(log)
            remaining = jnp.exp(last - wide[at, cols])
            values = x[at, cols].astype(F32)
            scaled = (values * remaining).astype(BF16)
            if 0 in wanted:
                new = jnp.dot(writer_t, scaled, preferred_element_type=F32)
                state[b, :, cols] = new
                if b == 0:
                    rows[p] = jnp.concatenate([last + log, last_dot + slope, jnp.zeros((6, 128), F32)], 0)
                    total[0, p] = (retain * new + state[1, :, cols]).astype(BF16)
            if 1 in wanted:
                scaled_dot = (
                    (x_dot[at, cols].astype(F32) + values * (last_dot - wide_dot[at, cols])) * remaining
                ).astype(BF16)
                new_dot = jnp.dot(writer_t, scaled_dot, preferred_element_type=F32) + jnp.dot(
                    writer_dot_t, scaled, preferred_element_type=F32
                )
                state_dot[b, :, cols] = new_dot
                if b == 0:
                    total[1, p] = (
                        retain * (new_dot + slope * state[0, :, cols]) + state_dot[1, :, cols]
                    ).astype(BF16)
            return 0

        lax.fori_loop(0, pairs, states, 0)

    def outer_t(left, right):
        return lax.dot_general(left, right, (((1,), (1,)), ((), ())), preferred_element_type=F32)

    def score_all(b):
        at = slice(b * SPAN, (b + 1) * SPAN)
        writer, reader = bc[at, 0:state_len], bc[at, state_len : 2 * state_len]
        writer_dot, reader_dot = bc_dot[at, 0:state_len], bc_dot[at, state_len : 2 * state_len]
        causal = t_index >= s_index
        score[b] = jnp.where(causal, outer_t(reader, writer), 0.0)
        score_dot[b] = jnp.where(causal, outer_t(reader_dot, writer) + outer_t(reader, writer_dot), 0.0)

    def mixing(b, p, _):
        cols = lanes(p * 128, 128)
        for t in range(SPAN // 128):
            size = (t + 1) * 128
            at = slice(b * SPAN + t * 128, b * SPAN + size)
            upto = slice(b * SPAN, b * SPAN + size)
            tile = slice(t * 128, size)
            values = x[upto, cols]
            both = jnp.concatenate([values, x_dot[upto, cols]], 1)
            column, column_dot = wide[at, cols], wide_dot[at, cols]
            found = []
            for k in range(2):
                first = k * HEAD_DIM
                row = cum_t[b, pl.ds(2 * p + k, 1), :][:, 0:size]
                row_dot = cum_dot_t[b, pl.ds(2 * p + k, 1), :][:, 0:size]
                weight = jnp.exp(jnp.minimum(column[:, first : first + 1] - row, 0.0))
                change = column_dot[:, first : first + 1] - row_dot
                scores = score[b, tile, 0:size]
                mix = (weight * scores).astype(BF16)
                mix_dot = (weight * (score_dot[b, tile, 0:size] + change * scores)).astype(BF16)
                found.append(
                    (
                        jnp.dot(mix, both, preferred_element_type=F32),
                        jnp.dot(mix_dot, values, preferred_element_type=F32),
                    )
                )
            (r0, q0), (r1, q1) = found
            within[at, cols] = jnp.where(lane < HEAD_DIM, r0[:, 0:128], r1[:, 0:128])
            within_dot[at, cols] = jnp.where(lane < HEAD_DIM, r0[:, 128:256] + q0, r1[:, 128:256] + q1)
        return 0

    halo_copies = [
        remote(
            proj.at[(k + 1) * length - 16 : (k + 1) * length, :],
            halo.at[k],
            halo_send.at[k],
            halo_recv.at[k],
            {"ctx": me + 1},
        )
        for k in range(2)
    ]
    out_half = p_near.shape[2]
    mine = odd * half
    others = (1 - odd) * half
    def pair_copy(source, into, k):
        return remote(source, into, pair_send.at[k], pair_recv.at[k], {"ctx": partner})

    pair_copies = [
        pair_copy(total.at[0, pl.ds(others, half)], pair_total.at[0], 0),
        pair_copy(rows.at[pl.ds(others, half)], pair_rows, 1),
        pair_copy(total.at[1, pl.ds(others, half)], pair_total.at[1], 2),
    ]
    chain_copies = [
        [
            remote(chain_out.at[k, i], chain_in.at[k, i], chain_send.at[k, i], chain_recv.at[k, i], {"ctx": me + 2})
            for i in range(half)
        ]
        for k in range(2)
    ]
    give_copies = [
        [
            remote(give.at[k, i], entry.at[k, mine + i], give_send.at[k, i], give_recv.at[k, i], {"ctx": partner})
            for i in range(half)
        ]
        for k in range(2)
    ]
    back_copies = [
        [
            remote(give.at[k, i], entry.at[k, others + i], give_send.at[k, i], give_recv.at[k, i], {"ctx": partner})
            for i in range(half)
        ]
        for k in range(2)
    ]
    first_here = odd == 0

    def ordered(own_part, their_part):
        return (
            jnp.where(first_here, own_part, their_part),
            jnp.where(first_here, their_part, own_part),
        )

    def link(k, i):
        @pl.when(me >= 2)
        def _():
            chain_copies[k][i].wait_recv()

        early_rows, late_rows = ordered(rows[mine + i], pair_rows[i])
        keep_early, keep_late = jnp.exp(early_rows[0:1]), jnp.exp(late_rows[0:1])
        early, late = ordered(total[0, mine + i].astype(F32), pair_total[0, i].astype(F32))
        arrived = chain_in[0, i].astype(F32)
        middle = keep_early * arrived + early
        leaving = keep_late * middle + late
        if k == 1:
            early, late = ordered(total[1, mine + i].astype(F32), pair_total[1, i].astype(F32))
            slope_early, slope_late = early_rows[1:2], late_rows[1:2]
            before = arrived
            arrived = chain_in[1, i].astype(F32)
            leaving = keep_early * (arrived + slope_early * before) + early
            leaving, middle = keep_late * (leaving + slope_late * middle) + late, leaving
        chain_out[k, i] = leaving.astype(BF16)

        @pl.when(me + 2 < count)
        def _():
            chain_copies[k][i].start()

        give[k, i] = jnp.where(first_here, middle, arrived).astype(BF16)
        give_copies[k][i].start()
        entry[k, mine + i] = jnp.where(first_here, arrived, middle).astype(BF16)

    def finish(p, _):
        cols = lanes(p * 128, 128)
        gain = wide[length : length + 1, cols]
        now = entry[0, p]
        for b in range(blocks):
            at = slice(b * SPAN, (b + 1) * SPAN)
            end = slice((b + 1) * SPAN - 1, (b + 1) * SPAN)
            read = jnp.dot(bc[at, state_len : 2 * state_len], now, preferred_element_type=F32)
            inner[at, cols] = (
                within[at, cols] + jnp.exp(wide[at, cols]) * read + gain * x[at, cols].astype(F32)
            ).astype(BF16)
            if b + 1 < blocks:
                now = (jnp.exp(wide[end, cols]) * now.astype(F32) + state[b, :, cols]).astype(BF16)
        return 0

    def finish_dot(p, _):
        cols = lanes(p * 128, 128)
        gain = wide[length : length + 1, cols]
        now, now_dot = entry[0, p], entry[1, p]
        for b in range(blocks):
            at = slice(b * SPAN, (b + 1) * SPAN)
            end = slice((b + 1) * SPAN - 1, (b + 1) * SPAN)
            reader = bc[at, state_len : 2 * state_len]
            reader_dot = bc_dot[at, state_len : 2 * state_len]
            read = jnp.dot(reader, jnp.concatenate([now, now_dot], 1), preferred_element_type=F32)
            moved = jnp.dot(reader_dot, now, preferred_element_type=F32)
            inner[length + b * SPAN : length + (b + 1) * SPAN, cols] = (
                within_dot[at, cols]
                + jnp.exp(wide[at, cols])
                * (read[:, 128:256] + moved + wide_dot[at, cols] * read[:, 0:128])
                + gain * x_dot[at, cols].astype(F32)
            ).astype(BF16)
            if b + 1 < blocks:
                retain = jnp.exp(wide[end, cols])
                old, old_dot = now.astype(F32), now_dot.astype(F32)
                now = (retain * old + state[b, :, cols]).astype(BF16)
                now_dot = (
                    retain * (old_dot + wide_dot[end, cols] * old) + state_dot[b, :, cols]
                ).astype(BF16)
        return 0

    keep = lanes(core * feat, feat)
    other_half = lanes((1 - core) * feat, feat)
    parts = 2 * length // SPAN

    def part(r):
        return slice(r * SPAN, (r + 1) * SPAN)

    a_copies = [
        remote(proj.at[part(r), other_half], r_far.at[r], a_send.at[r], a_recv.at[r], {"head": sib})
        for r in range(parts)
    ]
    x_copies = [
        remote(s_far.at[r], r_x.at[r], x_send.at[r], x_recv.at[r], {"head": far}) for r in range(parts)
    ]
    b_copies = [
        remote(p_near.at[r, :, other_half], r_near.at[r], b_send.at[r], b_recv.at[r], {"head": sib})
        for r in range(parts)
    ]

    def pass_on(r):
        a_copies[r].wait_recv()
        s_far[r] = (proj[part(r), keep].astype(F32) + r_far[r].astype(F32)).astype(BF16)
        x_copies[r].start()

    def far_terms(r):
        def one(j, _):
            cols = lanes(j * 256, 256)
            proj[part(r), cols] = jnp.dot(
                inner[part(r), :], weight[0:width, cols], preferred_element_type=F32
            ).astype(BF16)
            return 0

        lax.fori_loop(0, out_half // 256, one, 0)
        a_copies[r].start()

    def near_terms(r):
        def one(j, _):
            cols = lanes(j * 256, 256)
            p_near[r, :, cols] = jnp.dot(
                inner[part(r), :], weight[width : 2 * width, cols], preferred_element_type=F32
            ).astype(BF16)
            return 0

        lax.fori_loop(0, out_half // 256, one, 0)
        b_copies[r].start()

    for load in loads:
        load.wait()
    for c in (0, 1):
        near(c)
        forward(c)
        distant(c)

    @pl.when(me + 1 < count)
    def _():
        for copy in halo_copies:
            copy.start()

    convolve_all(1, (0, 1))
    states_all(1, (0, 1))
    score_all(1)
    lax.fori_loop(0, half, functools.partial(mixing, 1), 0)
    forward(2)
    lax.fori_loop(half, pairs, functools.partial(mixing, 1), 0)
    near(2)
    distant(2)

    @pl.when(me > 0)
    def _():
        for copy in halo_copies:
            copy.wait_recv()

    convolve_all(0, (0,))
    states_all(0, (0,))
    pair_copies[0].start()
    pair_copies[1].start()
    near(3)
    pair_copies[0].wait_recv()
    pair_copies[1].wait_recv()
    for i in range(half):
        link(0, i)
    forward(3)
    distant(3)

    w_far = weight.at[0:width, 0:out_half]
    w_near = weight.at[width : 2 * width, 0:out_half]
    load_far = pltpu.make_async_copy(w_out.at[:, lanes((1 - chip) * out_half, out_half)], w_far, w_sem.at[3])
    load_near = pltpu.make_async_copy(w_out.at[:, lanes(chip * out_half, out_half)], w_near, w_sem.at[4])
    load_far.start()
    load_near.start()

    convolve_all(0, (1,))
    states_all(0, (1,))
    pair_copies[2].start()
    score_all(0)
    lax.fori_loop(0, pairs, functools.partial(mixing, 0), 0)
    lax.fori_loop(mine, mine + half, finish, 0)
    load_far.wait()
    load_near.wait()

    @pl.when(me + 1 < count)
    def _():
        for copy in halo_copies:
            copy.wait_send()

    for i in range(half):
        back_copies[0][i].wait_recv()
    lax.fori_loop(others, others + half, finish, 0)
    far_terms(0)
    far_terms(1)
    pass_on(0)
    pair_copies[2].wait_recv()
    near_terms(0)
    pass_on(1)
    for i in range(half):
        link(1, i)
    lax.fori_loop(mine, mine + half, finish_dot, 0)
    for i in range(half):
        back_copies[1][i].wait_recv()
    lax.fori_loop(others, others + half, finish_dot, 0)
    far_terms(2)
    far_terms(3)
    pass_on(2)
    near_terms(1)
    pass_on(3)
    near_terms(2)
    near_terms(3)
    stores = [
        pltpu.make_async_copy(
            staged.at[r], (out if r < parts // 2 else out_dot).at[part(r % (parts // 2))], store_sem.at[r]
        )
        for r in range(parts)
    ]
    for r in range(parts):
        b_copies[r].wait_recv()
        x_copies[r].wait_recv()
        summed = p_near[r, :, keep].astype(F32) + r_near[r].astype(F32) + r_x[r].astype(F32)
        staged[r] = summed.astype(BF16)
        stores[r].start()

    for copy in far_copies + sib_copies + fwd_copies + pair_copies + give_copies[0] + give_copies[1]:
        copy.wait_send()
    for copy in a_copies + x_copies + b_copies:
        copy.wait_send()
    for store in stores:
        store.wait()

    @pl.when(me + 2 < count)
    def _():
        for copy in chain_copies[0] + chain_copies[1]:
            copy.wait_send()


def place_kernel(values, values_dot, out, out_dot, sem):
    size = out.shape[0] // 4
    copies = []
    for k, (source, into) in enumerate(((values, out), (values_dot, out_dot))):
        for i in range(4):
            at = slice(i * size, (i + 1) * size)
            copies.append(pltpu.make_async_copy(source.at[at], into.at[at], sem.at[4 * k + i]))
    for copy in copies:
        copy.start()
    for copy in copies:
        copy.wait()


def fused_on_device(
    tokens, tangent_tokens, log_decay, tangent_decay, w_inner, w_bmat, w_cmat,
    conv_inner, conv_bc, skip_gain, w_out,
):
    length, feat = tokens.shape
    depth, width = w_inner.shape
    state_len = w_bmat.shape[1]
    full = width + 2 * state_len
    out_half = w_out.shape[1] // 2
    blocks = length // SPAN
    parts = 2 * blocks
    pairs = width // 128
    half = pairs // 2
    vmem = pl.BlockSpec(memory_space=pltpu.VMEM)
    anywhere = pl.BlockSpec(memory_space=pl.ANY)
    dma = pltpu.SemaphoreType.DMA
    piece = (state_len, 128)

    def bf16(*shape):
        return pltpu.VMEM(shape, BF16)

    def f32(*shape):
        return pltpu.VMEM(shape, F32)

    result = jax.ShapeDtypeStruct((length, feat), BF16)
    outputs = pl.pallas_call(
        layer_kernel,
        out_shape=(result, result),
        in_specs=[anywhere] * 2 + [vmem] * 2 + [anywhere] * 3 + [vmem] * 3 + [anywhere],
        out_specs=(anywhere, anywhere),
        scratch_shapes=[
            bf16(3, 2 * length, feat),
            f32(SPAN + 16, full),
            bf16(depth, full),
            bf16(2 * length, full),
            bf16(2 * length, width),
            bf16(2, 16, full),
            f32(2, 16 + SPAN, 128),
            f32(2, 128, length),
            f32(length + 8, 128),
            f32(length, 128),
            f32(blocks, 128, SPAN),
            f32(blocks, 128, SPAN),
            f32(length + 8, width),
            f32(length, width),
            bf16(length, width),
            bf16(length, width),
            bf16(length, 2 * state_len),
            bf16(length, 2 * state_len),
            f32(blocks, SPAN, SPAN),
            f32(blocks, SPAN, SPAN),
            f32(length, width),
            f32(length, width),
            f32(blocks, state_len, width),
            f32(blocks, state_len, width),
            bf16(2, pairs, *piece),
            f32(pairs, 8, 128),
            bf16(2, half, *piece),
            f32(half, 8, 128),
            bf16(2, half, *piece),
            bf16(2, half, *piece),
            bf16(2, half, *piece),
            bf16(2, pairs, *piece),
            bf16(parts, SPAN, out_half),
        ]
        + [bf16(parts, SPAN, feat)] * 5
        + [bf16(length, feat)] * 2
        + [dma((parts,))]
        + [dma((7,))]
        + [dma((4,))] * 6
        + [dma((2,))] * 2
        + [dma((3,))] * 2
        + [dma((2, half))] * 4
        + [dma((parts,))] * 6,
        compiler_params=pltpu.CompilerParams(
            collective_id=0, has_side_effects=True, vmem_limit_bytes=VMEM_LIMIT
        ),
        name="layer",
    )(
        tokens, tangent_tokens, log_decay.T, tangent_decay.T, w_inner, w_bmat, w_cmat,
        conv_inner, conv_bc, skip_gain.reshape(1, -1), w_out,
    )
    return pl.pallas_call(
        place_kernel,
        out_shape=(result, result),
        in_specs=[anywhere, anywhere],
        out_specs=(anywhere, anywhere),
        scratch_shapes=[dma((8,))],
        compiler_params=pltpu.CompilerParams(vmem_limit_bytes=VMEM_LIMIT),
        name="place",
    )(*outputs)


def shifted(block, axis, distance):
    devices = range(lax.axis_size(axis))
    route = [(i - distance, i) for i in devices if i - distance in devices]
    return lax.ppermute(block, axis, route)


def carried_in(part, axis, combine, identity):
    place = lax.axis_index(axis)
    gathered = jax.tree.map(lambda a: lax.all_gather(a, axis), part)
    state = jax.tree.map(lambda a, e: jnp.zeros_like(a) + jnp.asarray(e, a.dtype), part, identity)

    def one(step, state):
        return combine(
            state, jax.tree.map(lambda a: lax.dynamic_index_in_dim(a, step, 0, False), gathered)
        )

    return lax.fori_loop(0, place, one, state)


def depthwise(padded, kernel):
    length = padded.shape[0] - kernel.shape[0] + 1
    summed = kernel[0] * padded[0:length]
    for offset in range(1, kernel.shape[0]):
        summed = summed + kernel[offset] * padded[offset : offset + length]
    return summed


def activate(values):
    return jax.nn.silu(values).astype(jnp.bfloat16)


def span_parts(inputs, writer, reader, decays):
    cumulative = jnp.cumsum(decays, axis=0)
    length = decays.shape[0]
    causal = lax.broadcasted_iota(jnp.int32, (length, length), 0) >= lax.broadcasted_iota(
        jnp.int32, (length, length), 1
    )
    differences = cumulative.T[:, :, None] - cumulative.T[:, None, :]
    weights = jnp.exp(jnp.where(causal[None], differences, -jnp.inf))
    scores = jnp.dot(reader, writer.T, preferred_element_type=jnp.float32)
    mixing = (weights * scores[None]).astype(jnp.bfloat16)
    within = jnp.einsum("hts,shp->thp", mixing, inputs, preferred_element_type=jnp.float32)
    remaining = jnp.exp(cumulative[-1][None, :] - cumulative)
    scaled = (inputs * remaining[:, :, None]).astype(jnp.bfloat16)
    block_state = jnp.einsum("shp,sn->hpn", scaled, writer, preferred_element_type=jnp.float32)
    return (cumulative, within, block_state)


def carried(reader, cumulative, initial):
    readout = jnp.einsum(
        "tn,hpn->thp", reader, initial.astype(jnp.bfloat16), preferred_element_type=jnp.float32
    )
    return jnp.exp(cumulative)[:, :, None] * readout


def combine(earlier, later):
    early_total, early_slope, early_state, early_tangent = earlier
    late_total, late_slope, late_state, late_tangent = later
    retain = jnp.exp(late_total)
    return (
        early_total + late_total,
        early_slope + late_slope,
        retain * early_state + late_state,
        retain * (early_tangent + late_slope * early_state) + late_tangent,
    )


def on_device(
    tokens,
    tangent_tokens,
    log_decay,
    tangent_decay,
    w_inner,
    w_bmat,
    w_cmat,
    conv_inner,
    conv_bc,
    skip_gain,
    w_out,
):
    length = tokens.shape[0]
    width = w_inner.shape[1]
    state_len = w_bmat.shape[1]
    heads_here = width // HEAD_DIM
    margin = conv_inner.shape[0] - 1
    blocks = length // SPAN
    stacked = jnp.concatenate([tokens, tangent_tokens], 0)
    shard_piece = lax.all_gather(stacked, "head", axis=1, tiled=True)
    sums = (
        jnp.dot(shard_piece, w_inner, preferred_element_type=jnp.float32),
        jnp.dot(shard_piece, w_bmat, preferred_element_type=jnp.float32),
        jnp.dot(shard_piece, w_cmat, preferred_element_type=jnp.float32),
    )
    projected = jnp.concatenate([summand.astype(jnp.bfloat16) for summand in sums], 1)
    edges = jnp.stack([projected[length - margin : length], projected[2 * length - margin :]])
    previous = shifted(edges, "ctx", 1)
    kernel = jnp.concatenate([conv_inner, conv_bc], 1)
    primal_conv = depthwise(jnp.concatenate([previous[0], projected[:length]], 0), kernel)
    tangent_conv = depthwise(jnp.concatenate([previous[1], projected[length:]], 0), kernel)
    mixed, mixed_dot = jax.jvp(activate, (primal_conv,), (tangent_conv,))

    def separate(values):
        inputs = values[:, :width].reshape(blocks, SPAN, heads_here, HEAD_DIM)
        writer = values[:, width : width + state_len].reshape(blocks, SPAN, state_len)
        reader = values[:, width + state_len :].reshape(blocks, SPAN, state_len)
        return (inputs, writer, reader)

    inputs, writer, reader = separate(mixed)
    inputs_dot, writer_dot, reader_dot = separate(mixed_dot)
    decays = log_decay.reshape(blocks, SPAN, heads_here)
    decays_dot = tangent_decay.reshape(blocks, SPAN, heads_here)
    (cumulative, within, block_state), (cumulative_dot, within_dot, block_dot) = jax.jvp(
        jax.vmap(span_parts),
        (inputs, writer, reader, decays),
        (inputs_dot, writer_dot, reader_dot, decays_dot),
    )

    def summarize(cumulative, block_state):
        summed = cumulative[0, -1]
        running = block_state[0]
        summed = summed + cumulative[1, -1]
        running = jnp.exp(cumulative[1, -1])[:, None, None] * running + block_state[1]
        return (summed[:, None, None], running)

    (decay_sum, own_state), (decay_sum_dot, own_dot) = jax.jvp(
        summarize, (cumulative, block_state), (cumulative_dot, block_dot)
    )
    message = (decay_sum, decay_sum_dot, own_state, own_dot)
    empty = tuple((jnp.zeros_like(member) for member in message))
    arriving = carried_in(message, "ctx", combine, empty)
    entry_state = arriving[2]
    entry_dot = arriving[3]

    def finish(initial, cumulative, within, block_state, inputs, reader):
        outputs = []
        for position in range(cumulative.shape[0]):
            combined = (
                within[position]
                + carried(reader[position], cumulative[position], initial)
                + skip_gain[None, :, None] * inputs[position]
            )
            outputs.append(combined.astype(jnp.bfloat16))
            if position + 1 < cumulative.shape[0]:
                initial = (
                    jnp.exp(cumulative[position, -1])[:, None, None] * initial
                    + block_state[position]
                )
        return jnp.stack(outputs)

    inner, inner_dot = jax.jvp(
        finish,
        (entry_state, cumulative, within, block_state, inputs, reader),
        (entry_dot, cumulative_dot, within_dot, block_dot, inputs_dot, reader_dot),
    )
    flattened = jnp.concatenate([inner.reshape(length, width), inner_dot.reshape(length, width)], 0)
    partial_term = jnp.dot(flattened, w_out, preferred_element_type=jnp.float32).astype(
        jnp.bfloat16
    )
    summed = (
        lax.psum_scatter(partial_term, "head", scatter_dimension=1, tiled=True)
        .astype(jnp.float32)
        .astype(jnp.bfloat16)
    )
    return (summed[:length], summed[length:])


def solution(mesh):
    in_specs = (
        P("ctx", "head"),
        P("ctx", "head"),
        P("ctx", "head"),
        P("ctx", "head"),
        P(None, "head"),
        P(),
        P(),
        P(None, "head"),
        P(),
        P("head"),
        P("head", None),
    )
    out_specs = (P("ctx", "head"), P("ctx", "head"))
    fits = mesh.shape["head"] == 4 and mesh.shape["ctx"] % 2 == 0
    return jax.shard_map(
        fused_on_device if fits else on_device, mesh=mesh, in_specs=in_specs, out_specs=out_specs, check_vma=False
    )
```

```python
import functools

import jax
import jax.numpy as jnp
from jax import lax
from jax.experimental import pallas as pl
from jax.experimental.pallas import tpu as pltpu
from jax.sharding import PartitionSpec as P

HEAD_DIM = 64
SPAN = 256
MESH = pl.DeviceIdType.MESH
HIGHEST = lax.Precision.HIGHEST
VMEM_LIMIT = 60 * 1024 * 1024
F32 = jnp.float32
BF16 = jnp.bfloat16


def remote(src, dst, send, recv, device):
    return pltpu.make_async_remote_copy(
        src_ref=src, dst_ref=dst, send_sem=send, recv_sem=recv, device_id=device, device_id_type=MESH
    )


def lanes(start, size):
    return pl.ds(pl.multiple_of(start, 128), size)


def layer_kernel(
    tok, tan, decay_t, decay_dot_t, w_in, w_b, w_c, conv_in, conv_bc, skip, w_out, out, out_dot,
    held, acc, weight, proj, inner,
    halo, padded, pad_dec, cum, cum_dot, cum_t, cum_dot_t, wide, wide_dot, x, x_dot, bc, bc_dot,
    score, score_dot, within, within_dot, state, state_dot,
    total, rows, pair_total, pair_rows, chain_in, chain_out, give, entry,
    p_near, r_far, s_far, r_x, r_near, staged, own_tok, own_tan,
    store_sem, w_sem, sib_send, sib_recv, far_send, far_recv, fwd_send, fwd_recv,
    halo_send, halo_recv, pair_send, pair_recv, chain_send, chain_recv, give_send, give_recv,
    a_send, a_recv, x_send, x_recv, b_send, b_recv,
):
    head = lax.axis_index("head")
    core = lax.rem(head, 2)
    chip = (head - core) // 2
    sib = head + 1 - 2 * core
    far = lax.rem(head + 2, 4)
    far_sib = lax.rem(sib + 2, 4)
    me = lax.axis_index("ctx")
    count = lax.axis_size("ctx")
    odd = lax.rem(me, 2)
    partner = me + 1 - 2 * odd
    length, feat = tok.shape
    width = x.shape[1]
    heads = decay_t.shape[0]
    pairs = width // 128
    half = pairs // 2
    blocks = length // SPAN
    state_len = bc.shape[1] // 2
    lane = lax.broadcasted_iota(jnp.int32, (1, 128), 1)

    loads = [
        pltpu.make_async_copy(tok, own_tok, w_sem.at[5]),
        pltpu.make_async_copy(tan, own_tan, w_sem.at[6]),
        pltpu.make_async_copy(w_in, weight.at[:, 0:width], w_sem.at[0]),
        pltpu.make_async_copy(w_b, weight.at[:, width : width + state_len], w_sem.at[1]),
        pltpu.make_async_copy(w_c, weight.at[:, width + state_len :], w_sem.at[2]),
    ]
    for load in loads:
        load.start()

    barrier = pltpu.get_barrier_semaphore()
    for other in (sib, far):
        pl.semaphore_signal(barrier, inc=1, device_id={"head": other}, device_id_type=MESH)
    for step in (-2, -1, 1, 2):
        other = me + step

        @pl.when(jnp.logical_and(other >= 0, other < count))
        def _(other=other):
            pl.semaphore_signal(barrier, inc=1, device_id={"ctx": other}, device_id_type=MESH)

    pl.semaphore_wait(barrier, 2 + jnp.minimum(me, 2) + jnp.minimum(count - 1 - me, 2))

    cut = length - SPAN - 16
    chunks = [(0, cut, length - cut), (1, cut, length - cut), (0, 0, cut), (1, 0, cut)]

    def own(c):
        k, start, size = chunks[c]
        return (tok, tan)[k].at[start : start + size]

    def own_values(c):
        k, start, size = chunks[c]
        return (own_tok, own_tan)[k][start : start + size, :]

    def span(c):
        k, start, size = chunks[c]
        return slice(k * length + start, k * length + start + size)

    order = range(len(chunks))
    far_copies = [
        remote(own(c), held.at[1, span(c)], far_send.at[c], far_recv.at[c], {"head": far}) for c in order
    ]
    sib_copies = [
        remote(own(c), held.at[0, span(c)], sib_send.at[c], sib_recv.at[c], {"head": sib}) for c in order
    ]
    fwd_copies = [
        remote(held.at[1, span(c)], held.at[2, span(c)], fwd_send.at[c], fwd_recv.at[c], {"head": sib})
        for c in order
    ]
    for c in order:
        far_copies[c].start()
        sib_copies[c].start()
    tiles = weight.shape[1] // 256

    def block(index):
        return pl.ds(pl.multiple_of(index * feat, 128), feat)

    def near(c):
        sib_copies[c].wait_recv()
        size = chunks[c][2]

        def one(j, _):
            cols = lanes(j * 256, 256)
            acc[0:size, cols] = jnp.dot(
                own_values(c), weight[block(head), cols], preferred_element_type=F32
            ) + jnp.dot(held[0, span(c), :], weight[block(sib), cols], preferred_element_type=F32)
            return 0

        lax.fori_loop(0, tiles, one, 0)

    def forward(c):
        far_copies[c].wait_recv()
        fwd_copies[c].start()

    def distant(c):
        size = chunks[c][2]

        def middle(j, _):
            cols = lanes(j * 256, 256)
            acc[0:size, cols] += jnp.dot(
                held[1, span(c), :], weight[block(far), cols], preferred_element_type=F32
            )
            return 0

        lax.fori_loop(0, tiles, middle, 0)
        fwd_copies[c].wait_recv()

        def last(j, _):
            cols = lanes(j * 256, 256)
            summed = acc[0:size, cols] + jnp.dot(
                held[2, span(c), :], weight[block(far_sib), cols], preferred_element_type=F32
            )
            proj[span(c), cols] = summed.astype(BF16)
            return 0

        lax.fori_loop(0, tiles, last, 0)

    @pl.when(me < 2)
    def _():
        chain_in[...] = jnp.zeros_like(chain_in)

    @pl.when(me == 0)
    def _():
        halo[...] = jnp.zeros_like(halo)

    pad_dec[...] = jnp.zeros_like(pad_dec)
    pad_dec[0, 0:heads, :] = decay_t[...]
    pad_dec[1, 0:heads, :] = decay_dot_t[...]
    t_index = lax.broadcasted_iota(jnp.int32, (SPAN, SPAN), 0)
    s_index = lax.broadcasted_iota(jnp.int32, (SPAN, SPAN), 1)
    upper = (t_index <= s_index).astype(F32)
    for b in range(blocks):
        at = slice(b * SPAN, (b + 1) * SPAN)
        for source, into, into_t in ((0, cum, cum_t), (1, cum_dot, cum_dot_t)):
            summed = jnp.dot(pad_dec[source, :, at], upper, precision=HIGHEST, preferred_element_type=F32)
            into_t[b] = summed
            into[at, :] = summed.T
    cum[length : length + 8, :] = jnp.zeros((8, 128), F32)
    cum[length : length + 1, 0:heads] = skip[...]

    def expand(p, _):
        cols = lanes(p * 128, 128)
        source = lax.broadcasted_iota(jnp.int32, (128, 128), 0)
        target = lax.broadcasted_iota(jnp.int32, (128, 128), 1)
        pick = (source == 2 * p + (target >= HEAD_DIM).astype(jnp.int32)).astype(F32)
        wide[:, cols] = jnp.dot(cum[...], pick, precision=HIGHEST, preferred_element_type=F32)
        wide_dot[:, cols] = jnp.dot(cum_dot[...], pick, precision=HIGHEST, preferred_element_type=F32)
        return 0

    lax.fori_loop(0, pairs, expand, 0)

    def convolve(b, wanted, cols, kernel, into, into_dot, to):
        start = b * SPAN
        convs = []
        for k in range(1 + max(wanted)):
            if b == 0:
                padded[k, 0:16, :] = halo[k, :, cols].astype(F32)
            else:
                padded[k, 0:16, :] = proj[k * length + start - 16 : k * length + start, cols].astype(F32)
            padded[k, 16 : 16 + SPAN, :] = proj[k * length + start : k * length + start + SPAN, cols].astype(F32)
            summed = kernel[0:1, :] * padded[k, 13 : 13 + SPAN, :]
            for tap in range(1, 4):
                summed = summed + kernel[tap : tap + 1, :] * padded[k, 13 + tap : 13 + tap + SPAN, :]
            convs.append(summed)
        gate = 1.0 / (1.0 + jnp.exp(-convs[0]))
        if 0 in wanted:
            into[start : start + SPAN, to] = (convs[0] * gate).astype(BF16)
        if 1 in wanted:
            into_dot[start : start + SPAN, to] = (
                convs[1] * (gate * (1.0 + convs[0] * (1.0 - gate)))
            ).astype(BF16)

    def convolve_all(b, wanted):
        for k in range(2):
            part = slice(k * state_len, (k + 1) * state_len)
            convolve(
                b, wanted, slice(width + k * state_len, width + (k + 1) * state_len), conv_bc[:, part], bc, bc_dot, part
            )

        def convolve_inner(p, _):
            cols = lanes(p * 128, 128)
            convolve(b, wanted, cols, conv_in[:, cols], x, x_dot, cols)
            return 0

        lax.fori_loop(0, pairs, convolve_inner, 0)

    def states_all(b, wanted):
        at = slice(b * SPAN, (b + 1) * SPAN)
        end = slice((b + 1) * SPAN - 1, (b + 1) * SPAN)
        final = slice(2 * SPAN - 1, 2 * SPAN)
        writer_t = bc[at, 0:state_len].T
        writer_dot_t = bc_dot[at, 0:state_len].T if 1 in wanted else None

        def states(p, _):
            cols = lanes(p * 128, 128)
            last, last_dot = wide[end, cols], wide_dot[end, cols]
            log, slope = wide[final, cols], wide_dot[final, cols]
            retain = jnp.exp(log)
            remaining = jnp.exp(last - wide[at, cols])
            values = x[at, cols].astype(F32)
            scaled = (values * remaining).astype(BF16)
            if 0 in wanted:
                new = jnp.dot(writer_t, scaled, preferred_element_type=F32)
                state[b, :, cols] = new
                if b == 0:
                    rows[p] = jnp.concatenate([last + log, last_dot + slope, jnp.zeros((6, 128), F32)], 0)
                    total[0, p] = (retain * new + state[1, :, cols]).astype(BF16)
            if 1 in wanted:
                scaled_dot = (
                    (x_dot[at, cols].astype(F32) + values * (last_dot - wide_dot[at, cols])) * remaining
                ).astype(BF16)
                new_dot = jnp.dot(writer_t, scaled_dot, preferred_element_type=F32) + jnp.dot(
                    writer_dot_t, scaled, preferred_element_type=F32
                )
                state_dot[b, :, cols] = new_dot
                if b == 0:
                    total[1, p] = (
                        retain * (new_dot + slope * state[0, :, cols]) + state_dot[1, :, cols]
                    ).astype(BF16)
            return 0

        lax.fori_loop(0, pairs, states, 0)

    def outer_t(left, right):
        return lax.dot_general(left, right, (((1,), (1,)), ((), ())), preferred_element_type=F32)

    def score_all(b):
        at = slice(b * SPAN, (b + 1) * SPAN)
        writer, reader = bc[at, 0:state_len], bc[at, state_len : 2 * state_len]
        writer_dot, reader_dot = bc_dot[at, 0:state_len], bc_dot[at, state_len : 2 * state_len]
        causal = t_index >= s_index
        score[b] = jnp.where(causal, outer_t(reader, writer), 0.0)
        score_dot[b] = jnp.where(causal, outer_t(reader_dot, writer) + outer_t(reader, writer_dot), 0.0)

    def mixing(b, p, _):
        cols = lanes(p * 128, 128)
        for t in range(SPAN // 128):
            size = (t + 1) * 128
            at = slice(b * SPAN + t * 128, b * SPAN + size)
            upto = slice(b * SPAN, b * SPAN + size)
            tile = slice(t * 128, size)
            values = x[upto, cols]
            both = jnp.concatenate([values, x_dot[upto, cols]], 1)
            column, column_dot = wide[at, cols], wide_dot[at, cols]
            found = []
            for k in range(2):
                first = k * HEAD_DIM
                row = cum_t[b, pl.ds(2 * p + k, 1), :][:, 0:size]
                row_dot = cum_dot_t[b, pl.ds(2 * p + k, 1), :][:, 0:size]
                weight = jnp.exp(jnp.minimum(column[:, first : first + 1] - row, 0.0))
                change = column_dot[:, first : first + 1] - row_dot
                scores = score[b, tile, 0:size]
                mix = (weight * scores).astype(BF16)
                mix_dot = (weight * (score_dot[b, tile, 0:size] + change * scores)).astype(BF16)
                found.append(
                    (
                        jnp.dot(mix, both, preferred_element_type=F32),
                        jnp.dot(mix_dot, values, preferred_element_type=F32),
                    )
                )
            (r0, q0), (r1, q1) = found
            within[at, cols] = jnp.where(lane < HEAD_DIM, r0[:, 0:128], r1[:, 0:128])
            within_dot[at, cols] = jnp.where(lane < HEAD_DIM, r0[:, 128:256] + q0, r1[:, 128:256] + q1)
        return 0

    halo_copies = [
        remote(
            proj.at[(k + 1) * length - 16 : (k + 1) * length, :],
            halo.at[k],
            halo_send.at[k],
            halo_recv.at[k],
            {"ctx": me + 1},
        )
        for k in range(2)
    ]
    out_half = p_near.shape[2]
    mine = odd * half
    others = (1 - odd) * half
    def pair_copy(source, into, k):
        return remote(source, into, pair_send.at[k], pair_recv.at[k], {"ctx": partner})

    pair_copies = [
        pair_copy(total.at[0, pl.ds(others, half)], pair_total.at[0], 0),
        pair_copy(rows.at[pl.ds(others, half)], pair_rows, 1),
        pair_copy(total.at[1, pl.ds(others, half)], pair_total.at[1], 2),
    ]
    chain_copies = [
        [
            remote(chain_out.at[k, i], chain_in.at[k, i], chain_send.at[k, i], chain_recv.at[k, i], {"ctx": me + 2})
            for i in range(half)
        ]
        for k in range(2)
    ]
    give_copies = [
        [
            remote(give.at[k, i], entry.at[k, mine + i], give_send.at[k, i], give_recv.at[k, i], {"ctx": partner})
            for i in range(half)
        ]
        for k in range(2)
    ]
    back_copies = [
        [
            remote(give.at[k, i], entry.at[k, others + i], give_send.at[k, i], give_recv.at[k, i], {"ctx": partner})
            for i in range(half)
        ]
        for k in range(2)
    ]
    first_here = odd == 0

    def ordered(own_part, their_part):
        return (
            jnp.where(first_here, own_part, their_part),
            jnp.where(first_here, their_part, own_part),
        )

    def link(k, i):
        @pl.when(me >= 2)
        def _():
            chain_copies[k][i].wait_recv()

        early_rows, late_rows = ordered(rows[mine + i], pair_rows[i])
        keep_early, keep_late = jnp.exp(early_rows[0:1]), jnp.exp(late_rows[0:1])
        early, late = ordered(total[0, mine + i].astype(F32), pair_total[0, i].astype(F32))
        arrived = chain_in[0, i].astype(F32)
        middle = keep_early * arrived + early
        leaving = keep_late * middle + late
        if k == 1:
            early, late = ordered(total[1, mine + i].astype(F32), pair_total[1, i].astype(F32))
            slope_early, slope_late = early_rows[1:2], late_rows[1:2]
            before = arrived
            arrived = chain_in[1, i].astype(F32)
            leaving = keep_early * (arrived + slope_early * before) + early
            leaving, middle = keep_late * (leaving + slope_late * middle) + late, leaving
        chain_out[k, i] = leaving.astype(BF16)

        @pl.when(me + 2 < count)
        def _():
            chain_copies[k][i].start()

        give[k, i] = jnp.where(first_here, middle, arrived).astype(BF16)
        give_copies[k][i].start()
        entry[k, mine + i] = jnp.where(first_here, arrived, middle).astype(BF16)

    def finish(p, _):
        cols = lanes(p * 128, 128)
        gain = wide[length : length + 1, cols]
        now = entry[0, p]
        for b in range(blocks):
            at = slice(b * SPAN, (b + 1) * SPAN)
            end = slice((b + 1) * SPAN - 1, (b + 1) * SPAN)
            read = jnp.dot(bc[at, state_len : 2 * state_len], now, preferred_element_type=F32)
            inner[at, cols] = (
                within[at, cols] + jnp.exp(wide[at, cols]) * read + gain * x[at, cols].astype(F32)
            ).astype(BF16)
            if b + 1 < blocks:
                now = (jnp.exp(wide[end, cols]) * now.astype(F32) + state[b, :, cols]).astype(BF16)
        return 0

    def finish_dot(p, _):
        cols = lanes(p * 128, 128)
        gain = wide[length : length + 1, cols]
        now, now_dot = entry[0, p], entry[1, p]
        for b in range(blocks):
            at = slice(b * SPAN, (b + 1) * SPAN)
            end = slice((b + 1) * SPAN - 1, (b + 1) * SPAN)
            reader = bc[at, state_len : 2 * state_len]
            reader_dot = bc_dot[at, state_len : 2 * state_len]
            read = jnp.dot(reader, jnp.concatenate([now, now_dot], 1), preferred_element_type=F32)
            moved = jnp.dot(reader_dot, now, preferred_element_type=F32)
            inner[length + b * SPAN : length + (b + 1) * SPAN, cols] = (
                within_dot[at, cols]
                + jnp.exp(wide[at, cols])
                * (read[:, 128:256] + moved + wide_dot[at, cols] * read[:, 0:128])
                + gain * x_dot[at, cols].astype(F32)
            ).astype(BF16)
            if b + 1 < blocks:
                retain = jnp.exp(wide[end, cols])
                old, old_dot = now.astype(F32), now_dot.astype(F32)
                now = (retain * old + state[b, :, cols]).astype(BF16)
                now_dot = (
                    retain * (old_dot + wide_dot[end, cols] * old) + state_dot[b, :, cols]
                ).astype(BF16)
        return 0

    keep = lanes(core * feat, feat)
    other_half = lanes((1 - core) * feat, feat)
    parts = 2 * length // SPAN

    def part(r):
        return slice(r * SPAN, (r + 1) * SPAN)

    a_copies = [
        remote(proj.at[part(r), other_half], r_far.at[r], a_send.at[r], a_recv.at[r], {"head": sib})
        for r in range(parts)
    ]
    x_copies = [
        remote(s_far.at[r], r_x.at[r], x_send.at[r], x_recv.at[r], {"head": far}) for r in range(parts)
    ]
    b_copies = [
        remote(p_near.at[r, :, other_half], r_near.at[r], b_send.at[r], b_recv.at[r], {"head": sib})
        for r in range(parts)
    ]

    def pass_on(r):
        a_copies[r].wait_recv()
        s_far[r] = (proj[part(r), keep].astype(F32) + r_far[r].astype(F32)).astype(BF16)
        x_copies[r].start()

    def far_terms(r):
        def one(j, _):
            cols = lanes(j * 256, 256)
            proj[part(r), cols] = jnp.dot(
                inner[part(r), :], weight[0:width, cols], preferred_element_type=F32
            ).astype(BF16)
            return 0

        lax.fori_loop(0, out_half // 256, one, 0)
        a_copies[r].start()

    def near_terms(r):
        def one(j, _):
            cols = lanes(j * 256, 256)
            p_near[r, :, cols] = jnp.dot(
                inner[part(r), :], weight[width : 2 * width, cols], preferred_element_type=F32
            ).astype(BF16)
            return 0

        lax.fori_loop(0, out_half // 256, one, 0)
        b_copies[r].start()

    for load in loads:
        load.wait()
    for c in (0, 1):
        near(c)
        forward(c)
        distant(c)

    @pl.when(me + 1 < count)
    def _():
        for copy in halo_copies:
            copy.start()

    convolve_all(1, (0, 1))
    states_all(1, (0, 1))
    score_all(1)
    lax.fori_loop(0, half, functools.partial(mixing, 1), 0)
    forward(2)
    lax.fori_loop(half, pairs, functools.partial(mixing, 1), 0)
    near(2)
    distant(2)

    @pl.when(me > 0)
    def _():
        for copy in halo_copies:
            copy.wait_recv()

    convolve_all(0, (0,))
    states_all(0, (0,))
    pair_copies[0].start()
    pair_copies[1].start()
    near(3)
    pair_copies[0].wait_recv()
    pair_copies[1].wait_recv()

    @pl.when(me < count // 2)
    def _():
        for i in range(half):
            link(0, i)

    forward(3)
    distant(3)

    w_far = weight.at[0:width, 0:out_half]
    w_near = weight.at[width : 2 * width, 0:out_half]
    load_far = pltpu.make_async_copy(w_out.at[:, lanes((1 - chip) * out_half, out_half)], w_far, w_sem.at[3])
    load_near = pltpu.make_async_copy(w_out.at[:, lanes(chip * out_half, out_half)], w_near, w_sem.at[4])
    load_far.start()
    load_near.start()

    convolve_all(0, (1,))
    states_all(0, (1,))
    pair_copies[2].start()

    @pl.when(me >= count // 2)
    def _():
        for i in range(half):
            link(0, i)

    score_all(0)
    lax.fori_loop(0, pairs, functools.partial(mixing, 0), 0)
    pair_copies[2].wait_recv()

    @pl.when(me < count // 2)
    def _():
        for i in range(half):
            link(1, i)

    lax.fori_loop(mine, mine + half, finish, 0)
    load_far.wait()
    load_near.wait()

    @pl.when(me + 1 < count)
    def _():
        for copy in halo_copies:
            copy.wait_send()

    for i in range(half):
        back_copies[0][i].wait_recv()
    lax.fori_loop(others, others + half, finish, 0)
    far_terms(0)
    far_terms(1)
    pass_on(0)
    near_terms(0)
    pass_on(1)

    @pl.when(me >= count // 2)
    def _():
        for i in range(half):
            link(1, i)

    lax.fori_loop(mine, mine + half, finish_dot, 0)
    for i in range(half):
        back_copies[1][i].wait_recv()
    lax.fori_loop(others, others + half, finish_dot, 0)
    far_terms(2)
    far_terms(3)
    pass_on(2)
    near_terms(1)
    pass_on(3)
    near_terms(2)
    near_terms(3)
    stores = [
        pltpu.make_async_copy(
            staged.at[r], (out if r < parts // 2 else out_dot).at[part(r % (parts // 2))], store_sem.at[r]
        )
        for r in range(parts)
    ]
    for r in range(parts):
        b_copies[r].wait_recv()
        x_copies[r].wait_recv()
        summed = p_near[r, :, keep].astype(F32) + r_near[r].astype(F32) + r_x[r].astype(F32)
        staged[r] = summed.astype(BF16)
        stores[r].start()

    for copy in far_copies + sib_copies + fwd_copies + pair_copies + give_copies[0] + give_copies[1]:
        copy.wait_send()
    for copy in a_copies + x_copies + b_copies:
        copy.wait_send()
    for store in stores:
        store.wait()

    @pl.when(me + 2 < count)
    def _():
        for copy in chain_copies[0] + chain_copies[1]:
            copy.wait_send()


def place_kernel(values, values_dot, out, out_dot, sem):
    size = out.shape[0] // 4
    copies = []
    for k, (source, into) in enumerate(((values, out), (values_dot, out_dot))):
        for i in range(4):
            at = slice(i * size, (i + 1) * size)
            copies.append(pltpu.make_async_copy(source.at[at], into.at[at], sem.at[4 * k + i]))
    for copy in copies:
        copy.start()
    for copy in copies:
        copy.wait()


def fused_on_device(
    tokens, tangent_tokens, log_decay, tangent_decay, w_inner, w_bmat, w_cmat,
    conv_inner, conv_bc, skip_gain, w_out,
):
    length, feat = tokens.shape
    depth, width = w_inner.shape
    state_len = w_bmat.shape[1]
    full = width + 2 * state_len
    out_half = w_out.shape[1] // 2
    blocks = length // SPAN
    parts = 2 * blocks
    pairs = width // 128
    half = pairs // 2
    vmem = pl.BlockSpec(memory_space=pltpu.VMEM)
    anywhere = pl.BlockSpec(memory_space=pl.ANY)
    dma = pltpu.SemaphoreType.DMA
    piece = (state_len, 128)

    def bf16(*shape):
        return pltpu.VMEM(shape, BF16)

    def f32(*shape):
        return pltpu.VMEM(shape, F32)

    result = jax.ShapeDtypeStruct((length, feat), BF16)
    outputs = pl.pallas_call(
        layer_kernel,
        out_shape=(result, result),
        in_specs=[anywhere] * 2 + [vmem] * 2 + [anywhere] * 3 + [vmem] * 3 + [anywhere],
        out_specs=(anywhere, anywhere),
        scratch_shapes=[
            bf16(3, 2 * length, feat),
            f32(SPAN + 16, full),
            bf16(depth, full),
            bf16(2 * length, full),
            bf16(2 * length, width),
            bf16(2, 16, full),
            f32(2, 16 + SPAN, 128),
            f32(2, 128, length),
            f32(length + 8, 128),
            f32(length, 128),
            f32(blocks, 128, SPAN),
            f32(blocks, 128, SPAN),
            f32(length + 8, width),
            f32(length, width),
            bf16(length, width),
            bf16(length, width),
            bf16(length, 2 * state_len),
            bf16(length, 2 * state_len),
            f32(blocks, SPAN, SPAN),
            f32(blocks, SPAN, SPAN),
            f32(length, width),
            f32(length, width),
            f32(blocks, state_len, width),
            f32(blocks, state_len, width),
            bf16(2, pairs, *piece),
            f32(pairs, 8, 128),
            bf16(2, half, *piece),
            f32(half, 8, 128),
            bf16(2, half, *piece),
            bf16(2, half, *piece),
            bf16(2, half, *piece),
            bf16(2, pairs, *piece),
            bf16(parts, SPAN, out_half),
        ]
        + [bf16(parts, SPAN, feat)] * 5
        + [bf16(length, feat)] * 2
        + [dma((parts,))]
        + [dma((7,))]
        + [dma((4,))] * 6
        + [dma((2,))] * 2
        + [dma((3,))] * 2
        + [dma((2, half))] * 4
        + [dma((parts,))] * 6,
        compiler_params=pltpu.CompilerParams(
            collective_id=0, has_side_effects=True, vmem_limit_bytes=VMEM_LIMIT
        ),
        name="layer",
    )(
        tokens, tangent_tokens, log_decay.T, tangent_decay.T, w_inner, w_bmat, w_cmat,
        conv_inner, conv_bc, skip_gain.reshape(1, -1), w_out,
    )
    return pl.pallas_call(
        place_kernel,
        out_shape=(result, result),
        in_specs=[anywhere, anywhere],
        out_specs=(vmem, vmem),
        scratch_shapes=[dma((8,))],
        compiler_params=pltpu.CompilerParams(vmem_limit_bytes=VMEM_LIMIT),
        name="place",
    )(*outputs)


def shifted(block, axis, distance):
    devices = range(lax.axis_size(axis))
    route = [(i - distance, i) for i in devices if i - distance in devices]
    return lax.ppermute(block, axis, route)


def carried_in(part, axis, combine, identity):
    place = lax.axis_index(axis)
    gathered = jax.tree.map(lambda a: lax.all_gather(a, axis), part)
    state = jax.tree.map(lambda a, e: jnp.zeros_like(a) + jnp.asarray(e, a.dtype), part, identity)

    def one(step, state):
        return combine(
            state, jax.tree.map(lambda a: lax.dynamic_index_in_dim(a, step, 0, False), gathered)
        )

    return lax.fori_loop(0, place, one, state)


def depthwise(padded, kernel):
    length = padded.shape[0] - kernel.shape[0] + 1
    summed = kernel[0] * padded[0:length]
    for offset in range(1, kernel.shape[0]):
        summed = summed + kernel[offset] * padded[offset : offset + length]
    return summed


def activate(values):
    return jax.nn.silu(values).astype(jnp.bfloat16)


def span_parts(inputs, writer, reader, decays):
    cumulative = jnp.cumsum(decays, axis=0)
    length = decays.shape[0]
    causal = lax.broadcasted_iota(jnp.int32, (length, length), 0) >= lax.broadcasted_iota(
        jnp.int32, (length, length), 1
    )
    differences = cumulative.T[:, :, None] - cumulative.T[:, None, :]
    weights = jnp.exp(jnp.where(causal[None], differences, -jnp.inf))
    scores = jnp.dot(reader, writer.T, preferred_element_type=jnp.float32)
    mixing = (weights * scores[None]).astype(jnp.bfloat16)
    within = jnp.einsum("hts,shp->thp", mixing, inputs, preferred_element_type=jnp.float32)
    remaining = jnp.exp(cumulative[-1][None, :] - cumulative)
    scaled = (inputs * remaining[:, :, None]).astype(jnp.bfloat16)
    block_state = jnp.einsum("shp,sn->hpn", scaled, writer, preferred_element_type=jnp.float32)
    return (cumulative, within, block_state)


def carried(reader, cumulative, initial):
    readout = jnp.einsum(
        "tn,hpn->thp", reader, initial.astype(jnp.bfloat16), preferred_element_type=jnp.float32
    )
    return jnp.exp(cumulative)[:, :, None] * readout


def combine(earlier, later):
    early_total, early_slope, early_state, early_tangent = earlier
    late_total, late_slope, late_state, late_tangent = later
    retain = jnp.exp(late_total)
    return (
        early_total + late_total,
        early_slope + late_slope,
        retain * early_state + late_state,
        retain * (early_tangent + late_slope * early_state) + late_tangent,
    )


def on_device(
    tokens,
    tangent_tokens,
    log_decay,
    tangent_decay,
    w_inner,
    w_bmat,
    w_cmat,
    conv_inner,
    conv_bc,
    skip_gain,
    w_out,
):
    length = tokens.shape[0]
    width = w_inner.shape[1]
    state_len = w_bmat.shape[1]
    heads_here = width // HEAD_DIM
    margin = conv_inner.shape[0] - 1
    blocks = length // SPAN
    stacked = jnp.concatenate([tokens, tangent_tokens], 0)
    shard_piece = lax.all_gather(stacked, "head", axis=1, tiled=True)
    sums = (
        jnp.dot(shard_piece, w_inner, preferred_element_type=jnp.float32),
        jnp.dot(shard_piece, w_bmat, preferred_element_type=jnp.float32),
        jnp.dot(shard_piece, w_cmat, preferred_element_type=jnp.float32),
    )
    projected = jnp.concatenate([summand.astype(jnp.bfloat16) for summand in sums], 1)
    edges = jnp.stack([projected[length - margin : length], projected[2 * length - margin :]])
    previous = shifted(edges, "ctx", 1)
    kernel = jnp.concatenate([conv_inner, conv_bc], 1)
    primal_conv = depthwise(jnp.concatenate([previous[0], projected[:length]], 0), kernel)
    tangent_conv = depthwise(jnp.concatenate([previous[1], projected[length:]], 0), kernel)
    mixed, mixed_dot = jax.jvp(activate, (primal_conv,), (tangent_conv,))

    def separate(values):
        inputs = values[:, :width].reshape(blocks, SPAN, heads_here, HEAD_DIM)
        writer = values[:, width : width + state_len].reshape(blocks, SPAN, state_len)
        reader = values[:, width + state_len :].reshape(blocks, SPAN, state_len)
        return (inputs, writer, reader)

    inputs, writer, reader = separate(mixed)
    inputs_dot, writer_dot, reader_dot = separate(mixed_dot)
    decays = log_decay.reshape(blocks, SPAN, heads_here)
    decays_dot = tangent_decay.reshape(blocks, SPAN, heads_here)
    (cumulative, within, block_state), (cumulative_dot, within_dot, block_dot) = jax.jvp(
        jax.vmap(span_parts),
        (inputs, writer, reader, decays),
        (inputs_dot, writer_dot, reader_dot, decays_dot),
    )

    def summarize(cumulative, block_state):
        summed = cumulative[0, -1]
        running = block_state[0]
        summed = summed + cumulative[1, -1]
        running = jnp.exp(cumulative[1, -1])[:, None, None] * running + block_state[1]
        return (summed[:, None, None], running)

    (decay_sum, own_state), (decay_sum_dot, own_dot) = jax.jvp(
        summarize, (cumulative, block_state), (cumulative_dot, block_dot)
    )
    message = (decay_sum, decay_sum_dot, own_state, own_dot)
    empty = tuple((jnp.zeros_like(member) for member in message))
    arriving = carried_in(message, "ctx", combine, empty)
    entry_state = arriving[2]
    entry_dot = arriving[3]

    def finish(initial, cumulative, within, block_state, inputs, reader):
        outputs = []
        for position in range(cumulative.shape[0]):
            combined = (
                within[position]
                + carried(reader[position], cumulative[position], initial)
                + skip_gain[None, :, None] * inputs[position]
            )
            outputs.append(combined.astype(jnp.bfloat16))
            if position + 1 < cumulative.shape[0]:
                initial = (
                    jnp.exp(cumulative[position, -1])[:, None, None] * initial
                    + block_state[position]
                )
        return jnp.stack(outputs)

    inner, inner_dot = jax.jvp(
        finish,
        (entry_state, cumulative, within, block_state, inputs, reader),
        (entry_dot, cumulative_dot, within_dot, block_dot, inputs_dot, reader_dot),
    )
    flattened = jnp.concatenate([inner.reshape(length, width), inner_dot.reshape(length, width)], 0)
    partial_term = jnp.dot(flattened, w_out, preferred_element_type=jnp.float32).astype(
        jnp.bfloat16
    )
    summed = (
        lax.psum_scatter(partial_term, "head", scatter_dimension=1, tiled=True)
        .astype(jnp.float32)
        .astype(jnp.bfloat16)
    )
    return (summed[:length], summed[length:])


def solution(mesh):
    in_specs = (
        P("ctx", "head"),
        P("ctx", "head"),
        P("ctx", "head"),
        P("ctx", "head"),
        P(None, "head"),
        P(),
        P(),
        P(None, "head"),
        P(),
        P("head"),
        P("head", None),
    )
    out_specs = (P("ctx", "head"), P("ctx", "head"))
    fits = mesh.shape["head"] == 4 and mesh.shape["ctx"] % 2 == 0
    return jax.shard_map(
        fused_on_device if fits else on_device, mesh=mesh, in_specs=in_specs, out_specs=out_specs, check_vma=False
    )
```
